128 devices in a mesh: row: 8 (over y_hi, x), col: 16 (over y_lo, z, core).
Axes of the slice: x: 4, y: 4 (y_hi: 2, y_lo: 2; y = y_hi * 2 + y_lo), z: 4, core: 2. Of those that a mesh axis runs over, the one named last changes fastest.
Arguments:
- homolog_features: bfloat16 [1024, 1024, 256], P(('row', 'col')), may hold values from -8 to 8
- presence_flags: int32 [1024, 1024], P(('row', 'col')), may hold values from 0 to 1, as said below
- residue_chain_index: int32 [1024], replicated, may hold values from 0 to 3, never falling along the last dimension, each value on 1 to 512 neighbouring positions
- pair_state: bfloat16 [1024, 1024, 128], P('row', 'col'), may hold values from -6 to 6
- standardize_scale: float32 [256], replicated, may hold values from 0.1 to 1.9
- standardize_shift: float32 [256], replicated, may hold values from -3 to 3
- left_factor_matrix: bfloat16 [256, 32], replicated, may hold values from -0.375 to 0.375
- right_factor_matrix: bfloat16 [256, 32], replicated, may hold values from -0.375 to 0.375
- output_weight: bfloat16 [1024, 128], replicated, may hold values from -0.1875 to 0.1875
- chain_pair_bias: float32 [2, 128], replicated, may hold values from -3 to 3
Outputs:
- pair_out: bfloat16 [1024, 1024, 128], P('row', 'col')
The draws below stay inside these ranges and needn't reach their ends.
Inputs may be any that keep to these rules, and one draw needn't show every extreme that they name: `presence_flags`: entries are 0 or 1; sequence 0, the query, is 1 at every residue. `residue_chain_index`: chain numbers never fall along the residues.
All inputs are finite; a program needn't handle non-finite values.
Results may differ from the reference program's by a relative error of at most 0.0036.
Values may be sent and summed in bfloat16 or wider, within the bound.
A program may use at most 128 MiB of HBM per device.

```python
import math
import jax
import jax.numpy as jnp
import numpy as np
from jax import lax

FEATURE_DEPTH = 256
C_Z = 128
PROJECTED_WIDTH = 32
SPAN_POSITIONS = 1024
CHAINS = 4
HOMOLOG_TOTAL = 1024


def draw_homolog_features(key, part):
    key = jax.random.fold_in(key, 11)
    random_key_motif, random_key_jitter = jax.random.split(key, 2)
    motif_template = jnp.clip(jax.random.normal(random_key_motif, (SPAN_POSITIONS, FEATURE_DEPTH), jnp.float32), -3.0, 3.0)
    jitter_draws = jnp.clip(jax.random.normal(random_key_jitter, (HOMOLOG_TOTAL, SPAN_POSITIONS, FEATURE_DEPTH), jnp.float32), -4.0, 4.0)
    return (motif_template + jitter_draws).astype(jnp.bfloat16)


def draw_presence_flags(key, part):
    key = jax.random.fold_in(key, 23)
    similarity_logits = jax.random.randint(key, (HOMOLOG_TOTAL, SPAN_POSITIONS), 0, 1000)
    feature_tiers = 900 - 600 * jnp.arange(HOMOLOG_TOTAL, dtype=jnp.int32) // HOMOLOG_TOTAL
    present = (similarity_logits < feature_tiers[:, None]).astype(jnp.int32)
    target_sequence = (jnp.arange(HOMOLOG_TOTAL, dtype=jnp.int32) == 0)[:, None]
    return jnp.where(target_sequence, 1, present).astype(jnp.int32)


def level_of(key, shape, shards, low, top_value):
    def one(position, blocks):
        steps = jax.random.uniform(jax.random.fold_in(jax.random.fold_in(key, 6), position), (blocks,), jnp.float32, low / len(shards), top_value / len(shards))
        return jnp.repeat(jnp.exp(steps), shape[position] // blocks).reshape((-1,) + (1,) * (len(shape) - position - 1))

    loudness = one(*shards[0])
    for cut in shards[1:]:
        loudness = loudness * one(*cut)
    return loudness


def profile(count, total, reach, skew):
    weights = [(1 << 20) // math.isqrt(standing ** skew) + 1 for standing in range(2, count + 1)]
    rest, given = total - reach - (count - 1), [1] * (count - 1)
    while rest > 0:
        free = [i for i in range(count - 1) if given[i] < reach]
        pool, budget = sum([weights[i] for i in free]), rest
        for i in free:
            addition = min(reach - given[i], max(1, budget * weights[i] // pool), rest)
            given[i] = given[i] + addition
            rest = rest - addition
    return np.array([reach] + given)


def ragged(key, number_of, total, limit, lean):
    if number_of == 2:
        one = jax.random.randint(key, (), max(1, total - limit), min(limit, total - 1) + 1)
        return jnp.stack([one, total - one])
    sizes = jnp.asarray(profile(number_of, total, limit, lean), jnp.int32)
    couples = (number_of - 1) // 2
    donor, receiver = sizes[1:1 + 2 * couples:2], sizes[2:2 + 2 * couples:2]
    room = jnp.minimum(donor - 1, limit - receiver)
    moved = jax.random.randint(jax.random.fold_in(key, 1), (couples,), 0, 1 << 20) % (room + 1)
    sizes = sizes.at[1:1 + 2 * couples:2].set(donor - moved).at[2:2 + 2 * couples:2].set(receiver + moved)
    return sizes[jax.random.permutation(jax.random.fold_in(key, 2), number_of)]


def normal_values(stream_key, shape, scale, most, shards=(), held_as=jnp.bfloat16):
    factor_of = level_of(stream_key, shape, shards, -0.22, 0.18) if shards else 1.0
    drawn = jax.random.normal(stream_key, shape, jnp.float32) * scale * factor_of
    return jnp.minimum(jnp.maximum(drawn, -most), most).astype(held_as)


def setup_inputs(seed: int = 0) -> dict:
    streams_of = jax.random.split(jax.random.key(seed), 11)
    homolog_features = draw_homolog_features(jax.random.fold_in(streams_of[10], 71), 0)
    presence_flags = draw_presence_flags(jax.random.fold_in(streams_of[10], 71), 0)
    residue_chain_index = jnp.searchsorted(jnp.cumsum(ragged(streams_of[2], CHAINS, SPAN_POSITIONS, SPAN_POSITIONS // 2, 0)), jnp.arange(SPAN_POSITIONS), side="right").astype(jnp.int32)
    pair_state = normal_values(streams_of[3], (SPAN_POSITIONS, SPAN_POSITIONS, C_Z), 1.0, 6.0, ((0, 8), (1, 16)))
    standardize_scale = jnp.clip(1.0 + 0.18 * jax.random.normal(streams_of[4], (FEATURE_DEPTH,), jnp.float32), 0.1, 1.9)
    standardize_shift = normal_values(streams_of[5], (FEATURE_DEPTH,), 0.5, 3.0, (), jnp.float32)
    left_factor_matrix = normal_values(streams_of[6], (FEATURE_DEPTH, PROJECTED_WIDTH), FEATURE_DEPTH ** -0.5, 0.375)
    right_factor_matrix = normal_values(streams_of[7], (FEATURE_DEPTH, PROJECTED_WIDTH), FEATURE_DEPTH ** -0.5, 0.375)
    output_weight = normal_values(streams_of[8], (PROJECTED_WIDTH * PROJECTED_WIDTH, C_Z), (PROJECTED_WIDTH * PROJECTED_WIDTH) ** -0.5, 0.1875)
    chain_pair_bias = normal_values(streams_of[9], (2, C_Z), 0.5, 3.0, (), jnp.float32)
    return {"homolog_features": homolog_features, "presence_flags": presence_flags, "residue_chain_index": residue_chain_index, "pair_state": pair_state, "standardize_scale": standardize_scale, "standardize_shift": standardize_shift, "left_factor_matrix": left_factor_matrix, "right_factor_matrix": right_factor_matrix, "output_weight": output_weight, "chain_pair_bias": chain_pair_bias}


def standardize_features(homolog_features, standardize_scale, standardize_shift):
    value_rows = homolog_features.astype(jnp.float32)
    centre = lax.optimization_barrier(jnp.mean(value_rows, axis=-1, keepdims=True))
    variance = lax.optimization_barrier(jnp.mean(jnp.square(value_rows - centre), axis=-1, keepdims=True))
    return ((value_rows - centre) * lax.rsqrt(variance + 1e-05) * standardize_scale + standardize_shift).astype(jnp.bfloat16)

def reference(homolog_features, presence_flags, residue_chain_index, pair_state, standardize_scale, standardize_shift, left_factor_matrix, right_factor_matrix, output_weight, chain_pair_bias):
    standardized_homologs = standardize_features(homolog_features, standardize_scale, standardize_shift).reshape(HOMOLOG_TOTAL * SPAN_POSITIONS, FEATURE_DEPTH)
    presence_real = presence_flags.astype(jnp.float32).reshape(HOMOLOG_TOTAL, SPAN_POSITIONS, 1)
    first_factor_vectors = (jnp.dot(standardized_homologs, left_factor_matrix, preferred_element_type=jnp.float32).reshape(HOMOLOG_TOTAL, SPAN_POSITIONS, PROJECTED_WIDTH) * presence_real).astype(jnp.bfloat16)
    second_factor_vectors = (jnp.dot(standardized_homologs, right_factor_matrix, preferred_element_type=jnp.float32).reshape(HOMOLOG_TOTAL, SPAN_POSITIONS, PROJECTED_WIDTH) * presence_real).astype(jnp.bfloat16)
    first_factor_masked = jnp.transpose(first_factor_vectors, (1, 2, 0)).reshape(SPAN_POSITIONS * PROJECTED_WIDTH, HOMOLOG_TOTAL)
    second_factor_masked = jnp.transpose(second_factor_vectors, (1, 2, 0)).reshape(SPAN_POSITIONS * PROJECTED_WIDTH, HOMOLOG_TOTAL)
    masked_rows = jnp.transpose(presence_flags).astype(jnp.float32)
    out_matrix = output_weight.astype(jnp.float32).reshape(PROJECTED_WIDTH, PROJECTED_WIDTH, C_Z)
    block_rows = min(64, SPAN_POSITIONS)

    def one_block(first):
        rows_here = lax.dynamic_slice_in_dim(first_factor_masked, first * PROJECTED_WIDTH, block_rows * PROJECTED_WIDTH, 0)
        outer_prod = jnp.dot(rows_here, second_factor_masked.T, preferred_element_type=jnp.float32).astype(jnp.bfloat16)
        outer_prod = lax.optimization_barrier(outer_prod)
        outer_prod = outer_prod.astype(jnp.float32).reshape(block_rows, PROJECTED_WIDTH, SPAN_POSITIONS, PROJECTED_WIDTH)
        update = jnp.einsum('icje,cez->ijz', outer_prod, out_matrix, precision=lax.Precision.HIGHEST)
        mask_here = lax.dynamic_slice_in_dim(masked_rows, first, block_rows, 0)
        counts = jnp.dot(mask_here, masked_rows.T, precision=lax.Precision.HIGHEST)
        return update / (counts[:, :, None] + 0.001)
    firsts = jnp.arange(SPAN_POSITIONS // block_rows, dtype=jnp.int32) * block_rows
    update = lax.map(one_block, firsts).reshape(SPAN_POSITIONS, SPAN_POSITIONS, C_Z)
    same_chain = (residue_chain_index[:, None] == residue_chain_index[None, :])[:, :, None]
    chain_term = jnp.where(same_chain, chain_pair_bias[0], chain_pair_bias[1])
    return (pair_state.astype(jnp.float32) + update + chain_term).astype(jnp.bfloat16)
```

```python
import jax
import jax.numpy as jnp
from jax import lax
from jax.experimental import pallas as pl
from jax.experimental.pallas import tpu as pltpu
from jax.sharding import PartitionSpec as P

MESH = pl.DeviceIdType.MESH
F32 = jnp.float32
BF16 = jnp.bfloat16
Q = 4
CJ = 16
NG = 2
MQ = 1


def kernel(
    feats, flags, chain_rows, chain_s, pair, scale, shift, wl, wr, wout, bias,
    out,
    F, Y, SB, RL, RR, L, Lm, R, SX, T, WT, PT, acc, CT, pair_v, out_v, bT,
    f_sem, p_sem, o_sem, a_ss, a_rl, a_rr, x_ss, x_rs, l_ss, l_rs, r_ss, r_rs,
):
    row = lax.axis_index("row")
    col = lax.axis_index("col")
    yh, x = row // 4, row % 4
    cc, core = col // 2, col % 2
    yl, z = cc // 4, cc % 4

    def dev(yh_, x_, yl_, z_, k_):
        return (yh_ * 4 + x_, yl_ * 8 + z_ * 2 + k_)

    def rc(src, dst, ss, rs, d):
        return pltpu.make_async_remote_copy(
            src_ref=src, dst_ref=dst, send_sem=ss, recv_sem=rs, device_id=d, device_id_type=MESH
        )

    bar = pltpu.get_barrier_semaphore()
    for n in range(8):
        for k in range(2):
            @pl.when(jnp.logical_not(jnp.logical_and(n == row, k == core)))
            def _():
                pl.semaphore_signal(bar, inc=1, device_id=(n, cc * 2 + k), device_id_type=MESH)
    for m in range(8):
        for k in range(2):
            @pl.when(m != cc)
            def _():
                pl.semaphore_signal(bar, inc=1, device_id=(row, m * 2 + k), device_id_type=MESH)

    def block_of(k):
        return lax.rem(row + cc + k, 8)

    def f_copy(k):
        b = block_of(k)
        return pltpu.make_async_copy(
            feats.at[:, pl.ds(pl.multiple_of(b * 128, 128), 128), :], F.at[k], f_sem.at[k]
        )

    for k in range(8):
        f_copy(k).start()
    p_copy = pltpu.make_async_copy(pair, pair_v, p_sem)
    p_copy.start()

    PT[...] = jnp.transpose(
        jnp.concatenate([wl[...].astype(F32), wr[...].astype(F32)], axis=1)
    ).astype(BF16)

    def project(k):
        b = block_of(k)
        present = flags[:, pl.ds(pl.multiple_of(b * 128, 128), 128)].astype(F32)
        for sp in range(4):
            v = F[k, 2 * sp:2 * sp + 2].reshape(256, 256).astype(F32)
            mu = jnp.mean(v, axis=-1, keepdims=True)
            d = v - mu
            var = jnp.mean(d * d, axis=-1, keepdims=True)
            nrm = (d * lax.rsqrt(var + 1e-05) * scale[...] + shift[...]).astype(BF16)
            pr = lax.dot_general(
                PT[...], nrm, (((1,), (1,)), ((), ())), preferred_element_type=F32
            )
            for u in range(2):
                s = 2 * sp + u
                Y[pl.ds(s, 64, stride=8), :] = pr[:, u * 128:(u + 1) * 128] * present[s:s + 1, :]
        pad = jnp.concatenate([present, jnp.zeros_like(present)], axis=0).astype(BF16)
        for h in range(2):
            for g in range(8):
                SB[b, h, 16 * g:16 * g + 16, :] = Y[(4 * g + 2 * h) * 8:(4 * g + 2 * h) * 8 + 16, :].astype(BF16)
            SB[b, 2 + h, 0:128, :] = Y[256 + h * 128:256 + (h + 1) * 128, :].astype(BF16)
            SB[b, h, 128:144, :] = pad
            SB[b, 2 + h, 128:144, :] = pad

    def scatter(k, wait):
        b = block_of(k)
        for h in range(2):
            mine = jnp.logical_and(b == row, h == core)
            left = rc(SB.at[b, h], RL.at[row, core], a_ss.at[k, h], a_rl.at[row, core], (b, cc * 2 + h))

            @pl.when(jnp.logical_not(mine))
            def _():
                left.wait_send() if wait else left.start()

            if not wait:
                @pl.when(mine)
                def _():
                    RL[row, core] = SB[b, h]

            mine_r = jnp.logical_and(b == cc, h == core)
            right = rc(SB.at[b, 2 + h], RR.at[cc, core], a_ss.at[k, 2 + h], a_rr.at[cc, core], (row, b * 2 + h))

            @pl.when(jnp.logical_not(mine_r))
            def _():
                right.wait_send() if wait else right.start()

            if not wait:
                @pl.when(mine_r)
                def _():
                    RR[cc, core] = SB[b, 2 + h]

    f_copy(0).wait()
    project(0)
    pl.semaphore_wait(bar, 29)
    scatter(0, False)

    def project_and_send(k, _):
        f_copy(k).wait()
        project(k)
        scatter(k, False)
        return 0

    lax.fori_loop(1, 8, project_and_send, 0)

    for g in range(8):
        WT[:, g * 128:(g + 1) * 128] = jnp.transpose(
            wout[g * 128:(g + 1) * 128, :].astype(F32)
        ).astype(BF16)
    bT[...] = jnp.transpose(
        jnp.concatenate([bias[...], jnp.zeros((126, 128), F32)], axis=0)
    )

    def clear(i, _):
        acc[i] = jnp.zeros((128, 256), F32)
        return 0

    lax.fori_loop(0, 32, clear, 0)

    for m in range(8):
        for k in range(2):
            @pl.when(jnp.logical_not(jnp.logical_and(m == cc, k == core)))
            def _():
                rc(RR.at[m, k], RR.at[m, k], a_ss.at[0, 0], a_rr.at[m, k], (row, col)).wait_recv()

    for ep in range(8):
        parts = [
            RR[m, k, 16 * ep:16 * ep + 16, :].astype(F32) for m in range(8) for k in range(2)
        ]
        for u in range(2):
            T[pl.ds(2 * ep + u, 128, stride=16), :] = jnp.transpose(
                jnp.concatenate([p[8 * u:8 * u + 8] for p in parts], axis=0)
            )
    e_half = pl.ds(pl.multiple_of(core * 16, 16), 16)
    SX[...] = T[pl.ds(pl.multiple_of((1 - core) * 1024, 1024), 1024), :].astype(BF16).reshape(64, 16, 128)
    sibling = dev(yh, x, yl, z, 1 - core)
    half_out = rc(SX, R.at[row, 2:66, e_half, :], x_ss, x_rs, sibling)
    half_out.start()
    R[row, 2:66, e_half, :] = T[pl.ds(pl.multiple_of(core * 1024, 1024), 1024), :].astype(BF16).reshape(64, 16, 128)
    mparts = jnp.concatenate(
        [RR[m, k, 128:144, :].astype(F32)[0:8] for m in range(8) for k in range(2)], axis=0
    )
    T[0:128, :] = jnp.transpose(mparts)
    R[row, 0:2] = T[pl.ds(pl.multiple_of(core * 64, 64), 64), :].astype(BF16).reshape(2, 32, 128)

    for n in range(8):
        for k in range(2):
            @pl.when(jnp.logical_not(jnp.logical_and(n == row, k == core)))
            def _():
                rc(RL.at[n, k], RL.at[n, k], a_ss.at[0, 0], a_rl.at[n, k], (row, col)).wait_recv()

    m_own = yl * 4 + z

    def rows_at(m):
        return pl.ds(pl.multiple_of(m * 16, 16), 16)

    def join(n, _):
        for g in range(8):
            a = RL[n, 0, 16 * g:16 * g + 16, :].astype(F32)
            b = RL[n, 1, 16 * g:16 * g + 16, :].astype(F32)
            for u in range(2):
                L[core, 2 * g + u, n, rows_at(m_own), :] = jnp.concatenate(
                    [a[8 * u:8 * u + 8], b[8 * u:8 * u + 8]], axis=0
                ).astype(BF16)
        return 0

    lax.fori_loop(0, 8, join, 0)
    for i in range(4):
        n = core * 4 + i
        a = RL[n, 0, 128:144, :].astype(F32)
        b = RL[n, 1, 128:144, :].astype(F32)
        Lm[n, rows_at(m_own), :] = jnp.concatenate([a[0:8], b[0:8]], axis=0).astype(BF16)

    sends = []

    def l_regions(q, h, m, half):
        lo, num = 2 * NG * q, 2 * NG
        n_lo, n_num = h * 4, 4
        if half is not None:
            num //= 2
            lo += half * num
            n_num //= 2
            n_lo = n_lo + half * n_num
        regions = [(q, L.at[h, lo:lo + num, :, rows_at(m), :])]
        if q == MQ:
            regions.append((Q, Lm.at[pl.ds(n_lo, n_num), rows_at(m), :]))
        return regions

    def l_send(q, m, half, to, slot):
        for i, ref in l_regions(q, core, m, half):
            c = rc(ref, ref, l_ss.at[i, slot], l_rs.at[i, slot], to)
            c.start()
            sends.append(c)

    def l_recv(q, h, m, half, slot):
        for i, ref in l_regions(q, h, m, half):
            rc(ref, ref, l_ss.at[i, slot], l_rs.at[i, slot], (row, col)).wait_recv()

    def r_region(p, n, half):
        lo = 0 if p == 0 else 2 + p * CJ
        num = CJ + 2 if p == 0 else CJ
        if half is not None:
            num //= 2
            lo += half * num
        return R.at[n, lo:lo + num]

    def r_send(p, n, half, to, slot):
        ref = r_region(p, n, half)
        c = rc(ref, ref, r_ss.at[p, slot], r_rs.at[p, slot], to)
        c.start()
        sends.append(c)

    def r_recv(p, n, half, slot):
        ref = r_region(p, n, half)
        rc(ref, ref, r_ss.at[p, slot], r_rs.at[p, slot], (row, col)).wait_recv()

    zu, zd, zo = lax.rem(z + 1, 4), lax.rem(z + 3, 4), lax.rem(z + 2, 4)
    xu, xd, xo = lax.rem(x + 1, 4), lax.rem(x + 3, 4), lax.rem(x + 2, 4)
    l_up, l_down = dev(yh, x, yl, zu, core), dev(yh, x, yl, zd, core)
    l_side = dev(yh, x, 1 - yl, z, core)
    r_up, r_down = dev(yh, xu, yl, z, core), dev(yh, xd, yl, z, core)
    r_side = dev(1 - yh, x, yl, z, core)
    ys = (yl, 1 - yl)
    hs = (yh, 1 - yh)

    def side(t):
        l_send(t, m_own, None, l_side, 0)
        r_send(t, row, None, r_side, 0)

    def first(t):
        l_send(t, m_own, None, l_up, 1)
        l_send(t, m_own, None, l_down, 2)
        r_send(t, row, None, r_up, 1)
        r_send(t, row, None, r_down, 2)
        l_send(t, m_own, None, sibling, 9)
        mp, np_ = ys[1] * 4 + z, hs[1] * 4 + x
        l_recv(t, core, mp, None, 0)
        l_send(t, mp, None, l_up, 3)
        l_send(t, mp, None, l_down, 4)
        r_recv(t, np_, None, 0)
        r_send(t, np_, None, r_up, 3)
        r_send(t, np_, None, r_down, 4)
        l_send(t, mp, None, sibling, 10)

    def second(t):
        for w in range(2):
            lu, ld = ys[w] * 4 + zu, ys[w] * 4 + zd
            ru, rd = hs[w] * 4 + xu, hs[w] * 4 + xd
            l_recv(t, core, ld, None, 1 + 2 * w)
            l_send(t, ld, 0, l_up, 5 + 2 * w)
            r_recv(t, rd, None, 1 + 2 * w)
            r_send(t, rd, 0, r_up, 5 + 2 * w)
            l_recv(t, core, lu, None, 2 + 2 * w)
            l_send(t, lu, 1, l_down, 6 + 2 * w)
            r_recv(t, ru, None, 2 + 2 * w)
            r_send(t, ru, 1, r_down, 6 + 2 * w)
            l_send(t, ld, None, sibling, 11 + 2 * w)
            l_send(t, lu, None, sibling, 12 + 2 * w)

    def third(t):
        for w in range(2):
            lo, ro = ys[w] * 4 + zo, hs[w] * 4 + xo
            l_recv(t, core, lo, 0, 5 + 2 * w)
            l_recv(t, core, lo, 1, 6 + 2 * w)
            l_send(t, lo, None, sibling, 15 + w)
            r_recv(t, ro, 0, 5 + 2 * w)
            r_recv(t, ro, 1, 6 + 2 * w)

    def fourth(t):
        for w in range(2):
            l_recv(t, 1 - core, ys[w] * 4 + z, None, 9 + w)
            l_recv(t, 1 - core, ys[w] * 4 + zd, None, 11 + 2 * w)
            l_recv(t, 1 - core, ys[w] * 4 + zu, None, 12 + 2 * w)
            l_recv(t, 1 - core, ys[w] * 4 + zo, None, 15 + w)

    def unit(q, p):
        lhs = jnp.concatenate(
            [R[n, pl.ds(2 + p * CJ, CJ)].reshape(CJ * 32, 128) for n in range(8)], axis=1
        )
        prods = []
        for gi in range(NG):
            for h in range(2):
                rhs = jnp.concatenate(
                    [L[h, (q * NG + gi) * 2 + u].reshape(1024, 128) for u in range(2)], axis=1
                )
                prods.append(jnp.dot(lhs, rhs, preferred_element_type=F32).astype(BF16))
        w = WT[:, pl.ds(pl.multiple_of(q * NG * 128, 128), NG * 128)]
        for jp in range(CJ // 2):
            blk = jnp.concatenate(
                [
                    jnp.concatenate(
                        [
                            o[j * 32:(j + 1) * 32, u * 128:(u + 1) * 128]
                            for o in prods for u in range(2)
                        ],
                        axis=0,
                    )
                    for j in (2 * jp, 2 * jp + 1)
                ],
                axis=1,
            )
            acc[p * (CJ // 2) + jp] += jnp.dot(w, blk, preferred_element_type=F32)

    def counts():
        total = jnp.zeros((64, 128), F32)
        for n in range(8):
            total = total + jnp.dot(
                R[n, 0:2].reshape(64, 128), Lm[n], preferred_element_type=F32
            )
        CT[...] = 1.0 / (total + 0.001)

    def out_copy(p):
        cols = pl.ds(pl.multiple_of(p * CJ, CJ), CJ)
        return pltpu.make_async_copy(out_v.at[:, cols, :], out.at[:, cols, :], o_sem.at[p])

    def finish(p):
        own = chain_rows[pl.ds(row, 1), :]
        for jp in range(CJ // 2):
            for u in range(2):
                j = 2 * jp + u
                a = acc[p * (CJ // 2) + jp, :, u * 128:(u + 1) * 128]
                a = a * CT[pl.ds(p * CJ + j, 1), :]
                same = own == chain_s[col * 64 + p * CJ + j]
                a = a + jnp.where(same, bT[:, 0:1], bT[:, 1:2])
                T[pl.ds(j, 128, stride=CJ), :] = jnp.transpose(a)
        cols = pl.ds(pl.multiple_of(p * CJ, CJ), CJ)
        out_v[:, cols, :] = (
            T[...].reshape(128, CJ, 128) + pair_v[:, cols, :].astype(F32)
        ).astype(BF16)
        out_copy(p).start()

    def compute(t):
        if t < Q - 1:
            if t > 0:
                lax.fori_loop(0, t, lambda q, _: (unit(q, t), 0)[1], 0)
            lax.fori_loop(0, t + 1, lambda p, _: (unit(t, p), 0)[1], 0)
        else:
            lax.fori_loop(0, t, lambda q, _: (unit(q, t), 0)[1], 0)
            counts()
            p_copy.wait()

            def last(p, _):
                unit(t, p)
                finish(p)
                return 0

            lax.fori_loop(0, Q, last, 0)

    rc(SX, R.at[row, 2:66, pl.ds(pl.multiple_of((1 - core) * 16, 16), 16), :], x_ss, x_rs, sibling).wait_recv()
    side(0)
    for t in range(Q + 2):
        if t + 1 < Q:
            side(t + 1)
        if t < Q:
            first(t)
        if 1 <= t <= Q:
            second(t - 1)
        if t >= 2:
            compute(t - 2)
        if 1 <= t <= Q:
            third(t - 1)
            fourth(t - 1)

    for c in sends:
        c.wait_send()
    half_out.wait_send()
    for k in range(8):
        scatter(k, True)
    for p in range(Q):
        out_copy(p).wait()


def per_device(
    homolog_features,
    presence_flags,
    residue_chain_index,
    pair_state,
    standardize_scale,
    standardize_shift,
    left_factor_matrix,
    right_factor_matrix,
    output_weight,
    chain_pair_bias,
):
    anywhere = pl.BlockSpec(memory_space=pl.ANY)
    vmem = pl.BlockSpec(memory_space=pltpu.VMEM)
    smem = pl.BlockSpec(memory_space=pltpu.SMEM)
    dma = pltpu.SemaphoreType.DMA
    return pl.pallas_call(
        kernel,
        out_shape=jax.ShapeDtypeStruct(pair_state.shape, BF16),
        in_specs=[anywhere, vmem, vmem, smem, anywhere, vmem, vmem, vmem, vmem, vmem, vmem],
        out_specs=anywhere,
        scratch_shapes=[
            pltpu.VMEM((8, 8, 128, 256), BF16),
            pltpu.VMEM((512, 128), F32),
            pltpu.VMEM((8, 4, 144, 128), BF16),
            pltpu.VMEM((8, 2, 144, 128), BF16),
            pltpu.VMEM((8, 2, 144, 128), BF16),
            pltpu.VMEM((2, 16, 8, 128, 128), BF16),
            pltpu.VMEM((8, 128, 128), BF16),
            pltpu.VMEM((8, 66, 32, 128), BF16),
            pltpu.VMEM((64, 16, 128), BF16),
            pltpu.VMEM((2048, 128), F32),
            pltpu.VMEM((128, 1024), BF16),
            pltpu.VMEM((64, 256), BF16),
            pltpu.VMEM((32, 128, 256), F32),
            pltpu.VMEM((64, 128), F32),
            pltpu.VMEM((128, 64, 128), BF16),
            pltpu.VMEM((128, 64, 128), BF16),
            pltpu.VMEM((128, 128), F32),
            dma((8,)), dma(()), dma((Q,)),
            dma((8, 4)), dma((8, 2)), dma((8, 2)), dma(()), dma(()),
            dma((Q + 1, 17)), dma((Q + 1, 17)), dma((Q, 9)), dma((Q, 9)),
        ],
        compiler_params=pltpu.CompilerParams(
            collective_id=0, has_side_effects=True, vmem_limit_bytes=60 << 20
        ),
    )(
        homolog_features, presence_flags, residue_chain_index.reshape(8, 128),
        residue_chain_index, pair_state, standardize_scale.reshape(1, -1),
        standardize_shift.reshape(1, -1), left_factor_matrix, right_factor_matrix,
        output_weight, chain_pair_bias,
    )


def solution(mesh):
    return jax.shard_map(
        per_device,
        mesh=mesh,
        in_specs=(
            P(("row", "col"), None, None),
            P(("row", "col"), None),
            P(),
            P("row", "col", None),
            P(),
            P(),
            P(),
            P(),
            P(),
            P(),
        ),
        out_specs=P("row", "col", None),
        check_vma=False,
    )
```

```python
import jax
import jax.numpy as jnp
from jax import lax
from jax.experimental import pallas as pl
from jax.experimental.pallas import tpu as pltpu
from jax.sharding import PartitionSpec as P

MESH = pl.DeviceIdType.MESH
F32 = jnp.float32
BF16 = jnp.bfloat16
Q = 4
CJ = 16
NG = 2
MQ = 1


def kernel(
    feats, flags, chain_rows, chain_s, pair, scale, shift, wl, wr, wout, bias,
    out,
    F, Y, SB, RL, RR, L, Lm, R, SX, T, WT, PT, acc, CT, pair_v, out_v, bT,
    f_sem, p_sem, o_sem, a_ss, a_rl, a_rr, x_ss, x_rs, l_ss, l_rs, r_ss, r_rs,
):
    row = lax.axis_index("row")
    col = lax.axis_index("col")
    yh, x = row // 4, row % 4
    cc, core = col // 2, col % 2
    yl, z = cc // 4, cc % 4

    def dev(yh_, x_, yl_, z_, k_):
        return (yh_ * 4 + x_, yl_ * 8 + z_ * 2 + k_)

    def rc(src, dst, ss, rs, d):
        return pltpu.make_async_remote_copy(
            src_ref=src, dst_ref=dst, send_sem=ss, recv_sem=rs, device_id=d, device_id_type=MESH
        )

    bar = pltpu.get_barrier_semaphore()
    for n in range(8):
        for k in range(2):
            @pl.when(jnp.logical_not(jnp.logical_and(n == row, k == core)))
            def _():
                pl.semaphore_signal(bar, inc=1, device_id=(n, cc * 2 + k), device_id_type=MESH)
    for m in range(8):
        for k in range(2):
            @pl.when(m != cc)
            def _():
                pl.semaphore_signal(bar, inc=1, device_id=(row, m * 2 + k), device_id_type=MESH)

    def block_of(k):
        return lax.rem(row + cc + k, 8)

    def f_copy(k):
        b = block_of(k)
        return pltpu.make_async_copy(
            feats.at[:, pl.ds(pl.multiple_of(b * 128, 128), 128), :], F.at[k], f_sem.at[k]
        )

    for k in range(8):
        f_copy(k).start()
    p_copy = pltpu.make_async_copy(pair, pair_v, p_sem)
    p_copy.start()

    PT[0:32, :] = wl[...]
    PT[32:64, :] = wr[...]

    def project(k):
        b = block_of(k)
        present = flags[:, pl.ds(pl.multiple_of(b * 128, 128), 128)].astype(F32)
        for sp in range(4):
            v = F[k, 2 * sp:2 * sp + 2].reshape(256, 256).astype(F32)
            mu = jnp.mean(v, axis=-1, keepdims=True)
            d = v - mu
            var = jnp.mean(d * d, axis=-1, keepdims=True)
            nrm = (d * lax.rsqrt(var + 1e-05) * scale[...] + shift[...]).astype(BF16)
            pr = lax.dot_general(
                PT[...], nrm, (((1,), (1,)), ((), ())), preferred_element_type=F32
            )
            for u in range(2):
                s = 2 * sp + u
                Y[pl.ds(s, 64, stride=8), :] = pr[:, u * 128:(u + 1) * 128] * present[s:s + 1, :]
        pad = jnp.concatenate([present, jnp.zeros_like(present)], axis=0).astype(BF16)
        for h in range(2):
            for g in range(8):
                SB[b, h, 16 * g:16 * g + 16, :] = Y[(4 * g + 2 * h) * 8:(4 * g + 2 * h) * 8 + 16, :].astype(BF16)
            SB[b, 2 + h, 0:128, :] = Y[256 + h * 128:256 + (h + 1) * 128, :].astype(BF16)
            SB[b, h, 128:144, :] = pad
            SB[b, 2 + h, 128:144, :] = pad

    def scatter(k, wait):
        b = block_of(k)
        for h in range(2):
            mine = jnp.logical_and(b == row, h == core)
            left = rc(SB.at[b, h], RL.at[row, core], a_ss.at[k, h], a_rl.at[row, core], (b, cc * 2 + h))

            @pl.when(jnp.logical_not(mine))
            def _():
                left.wait_send() if wait else left.start()

            if not wait:
                @pl.when(mine)
                def _():
                    RL[row, core] = SB[b, h]

            mine_r = jnp.logical_and(b == cc, h == core)
            right = rc(SB.at[b, 2 + h], RR.at[cc, core], a_ss.at[k, 2 + h], a_rr.at[cc, core], (row, b * 2 + h))

            @pl.when(jnp.logical_not(mine_r))
            def _():
                right.wait_send() if wait else right.start()

            if not wait:
                @pl.when(mine_r)
                def _():
                    RR[cc, core] = SB[b, 2 + h]

    def project_block(k, _):
        f_copy(k).wait()
        project(k)
        return 0

    lax.fori_loop(0, 8, project_block, 0)
    pl.semaphore_wait(bar, 29)
    lax.fori_loop(0, 8, lambda k, _: (scatter(k, False), 0)[1], 0)

    for g in range(8):
        WT[:, g * 128:(g + 1) * 128] = jnp.transpose(
            wout[g * 128:(g + 1) * 128, :].astype(F32)
        ).astype(BF16)
    bT[...] = jnp.transpose(
        jnp.concatenate([bias[...], jnp.zeros((126, 128), F32)], axis=0)
    )

    def clear(i, _):
        acc[i] = jnp.zeros((128, 256), F32)
        return 0

    lax.fori_loop(0, 32, clear, 0)

    for m in range(8):
        for k in range(2):
            @pl.when(jnp.logical_not(jnp.logical_and(m == cc, k == core)))
            def _():
                rc(RR.at[m, k], RR.at[m, k], a_ss.at[0, 0], a_rr.at[m, k], (row, col)).wait_recv()

    for ep in range(8):
        parts = [
            RR[m, k, 16 * ep:16 * ep + 16, :].astype(F32) for m in range(8) for k in range(2)
        ]
        for u in range(2):
            T[pl.ds(2 * ep + u, 128, stride=16), :] = jnp.transpose(
                jnp.concatenate([p[8 * u:8 * u + 8] for p in parts], axis=0)
            )
    e_half = pl.ds(pl.multiple_of(core * 16, 16), 16)
    SX[...] = T[pl.ds(pl.multiple_of((1 - core) * 1024, 1024), 1024), :].astype(BF16).reshape(64, 16, 128)
    sibling = dev(yh, x, yl, z, 1 - core)
    half_out = rc(SX, R.at[row, 2:66, e_half, :], x_ss, x_rs, sibling)
    half_out.start()
    R[row, 2:66, e_half, :] = T[pl.ds(pl.multiple_of(core * 1024, 1024), 1024), :].astype(BF16).reshape(64, 16, 128)
    mparts = jnp.concatenate(
        [RR[m, k, 128:144, :].astype(F32)[0:8] for m in range(8) for k in range(2)], axis=0
    )
    T[0:128, :] = jnp.transpose(mparts)
    R[row, 0:2] = T[pl.ds(pl.multiple_of(core * 64, 64), 64), :].astype(BF16).reshape(2, 32, 128)

    for n in range(8):
        for k in range(2):
            @pl.when(jnp.logical_not(jnp.logical_and(n == row, k == core)))
            def _():
                rc(RL.at[n, k], RL.at[n, k], a_ss.at[0, 0], a_rl.at[n, k], (row, col)).wait_recv()

    m_own = yl * 4 + z

    def rows_at(m):
        return pl.ds(pl.multiple_of(m * 16, 16), 16)

    def join(n, _):
        for g in range(8):
            a = RL[n, 0, 16 * g:16 * g + 16, :].astype(F32)
            b = RL[n, 1, 16 * g:16 * g + 16, :].astype(F32)
            for u in range(2):
                L[core, 2 * g + u, n, rows_at(m_own), :] = jnp.concatenate(
                    [a[8 * u:8 * u + 8], b[8 * u:8 * u + 8]], axis=0
                ).astype(BF16)
        return 0

    lax.fori_loop(0, 8, join, 0)
    for i in range(4):
        n = core * 4 + i
        a = RL[n, 0, 128:144, :].astype(F32)
        b = RL[n, 1, 128:144, :].astype(F32)
        Lm[n, rows_at(m_own), :] = jnp.concatenate([a[0:8], b[0:8]], axis=0).astype(BF16)

    sends = []

    def l_regions(q, h, m, half):
        lo, num = 2 * NG * q, 2 * NG
        n_lo, n_num = h * 4, 4
        if half is not None:
            num //= 2
            lo += half * num
            n_num //= 2
            n_lo = n_lo + half * n_num
        regions = [(q, L.at[h, lo:lo + num, :, rows_at(m), :])]
        if q == MQ:
            regions.append((Q, Lm.at[pl.ds(n_lo, n_num), rows_at(m), :]))
        return regions

    def l_send(q, m, half, to, slot):
        for i, ref in l_regions(q, core, m, half):
            c = rc(ref, ref, l_ss.at[i, slot], l_rs.at[i, slot], to)
            c.start()
            sends.append(c)

    def l_recv(q, h, m, half, slot):
        for i, ref in l_regions(q, h, m, half):
            rc(ref, ref, l_ss.at[i, slot], l_rs.at[i, slot], (row, col)).wait_recv()

    def r_region(p, n, half):
        lo = 0 if p == 0 else 2 + p * CJ
        num = CJ + 2 if p == 0 else CJ
        if half is not None:
            num //= 2
            lo += half * num
        return R.at[n, lo:lo + num]

    def r_send(p, n, half, to, slot):
        ref = r_region(p, n, half)
        c = rc(ref, ref, r_ss.at[p, slot], r_rs.at[p, slot], to)
        c.start()
        sends.append(c)

    def r_recv(p, n, half, slot):
        ref = r_region(p, n, half)
        rc(ref, ref, r_ss.at[p, slot], r_rs.at[p, slot], (row, col)).wait_recv()

    zu, zd, zo = lax.rem(z + 1, 4), lax.rem(z + 3, 4), lax.rem(z + 2, 4)
    xu, xd, xo = lax.rem(x + 1, 4), lax.rem(x + 3, 4), lax.rem(x + 2, 4)
    l_up, l_down = dev(yh, x, yl, zu, core), dev(yh, x, yl, zd, core)
    l_side = dev(yh, x, 1 - yl, z, core)
    r_up, r_down = dev(yh, xu, yl, z, core), dev(yh, xd, yl, z, core)
    r_side = dev(1 - yh, x, yl, z, core)
    ys = (yl, 1 - yl)
    hs = (yh, 1 - yh)

    def side(t):
        l_send(t, m_own, None, l_side, 0)
        r_send(t, row, None, r_side, 0)

    def first(t):
        l_send(t, m_own, None, l_up, 1)
        l_send(t, m_own, None, l_down, 2)
        r_send(t, row, None, r_up, 1)
        r_send(t, row, None, r_down, 2)
        l_send(t, m_own, None, sibling, 9)

    def partner(t):
        mp, np_ = ys[1] * 4 + z, hs[1] * 4 + x
        l_recv(t, core, mp, None, 0)
        l_send(t, mp, None, l_up, 3)
        l_send(t, mp, None, l_down, 4)
        r_recv(t, np_, None, 0)
        r_send(t, np_, None, r_up, 3)
        r_send(t, np_, None, r_down, 4)
        l_send(t, mp, None, sibling, 10)

    def second(t):
        for w in range(2):
            lu, ld = ys[w] * 4 + zu, ys[w] * 4 + zd
            ru, rd = hs[w] * 4 + xu, hs[w] * 4 + xd
            l_recv(t, core, ld, None, 1 + 2 * w)
            l_send(t, ld, 0, l_up, 5 + 2 * w)
            r_recv(t, rd, None, 1 + 2 * w)
            r_send(t, rd, 0, r_up, 5 + 2 * w)
            l_recv(t, core, lu, None, 2 + 2 * w)
            l_send(t, lu, 1, l_down, 6 + 2 * w)
            r_recv(t, ru, None, 2 + 2 * w)
            r_send(t, ru, 1, r_down, 6 + 2 * w)
            l_send(t, ld, None, sibling, 11 + 2 * w)
            l_send(t, lu, None, sibling, 12 + 2 * w)

    def third(t):
        for w in range(2):
            lo, ro = ys[w] * 4 + zo, hs[w] * 4 + xo
            l_recv(t, core, lo, 0, 5 + 2 * w)
            l_recv(t, core, lo, 1, 6 + 2 * w)
            l_send(t, lo, None, sibling, 15 + w)
            r_recv(t, ro, 0, 5 + 2 * w)
            r_recv(t, ro, 1, 6 + 2 * w)

    def fourth(t):
        for w in range(2):
            l_recv(t, 1 - core, ys[w] * 4 + z, None, 9 + w)
            l_recv(t, 1 - core, ys[w] * 4 + zd, None, 11 + 2 * w)
            l_recv(t, 1 - core, ys[w] * 4 + zu, None, 12 + 2 * w)
            l_recv(t, 1 - core, ys[w] * 4 + zo, None, 15 + w)

    def unit(q, p):
        lhs = jnp.concatenate(
            [R[n, pl.ds(2 + p * CJ, CJ)].reshape(CJ * 32, 128) for n in range(8)], axis=1
        )
        prods = []
        for gi in range(NG):
            for h in range(2):
                rhs = jnp.concatenate(
                    [L[h, (q * NG + gi) * 2 + u].reshape(1024, 128) for u in range(2)], axis=1
                )
                prods.append(jnp.dot(lhs, rhs, preferred_element_type=F32).astype(BF16))
        w = WT[:, pl.ds(pl.multiple_of(q * NG * 128, 128), NG * 128)]
        for jp in range(CJ // 2):
            blk = jnp.concatenate(
                [
                    jnp.concatenate(
                        [
                            o[j * 32:(j + 1) * 32, u * 128:(u + 1) * 128]
                            for o in prods for u in range(2)
                        ],
                        axis=0,
                    )
                    for j in (2 * jp, 2 * jp + 1)
                ],
                axis=1,
            )
            acc[p * (CJ // 2) + jp] += jnp.dot(w, blk, preferred_element_type=F32)

    def counts():
        total = jnp.zeros((64, 128), F32)
        for n in range(8):
            total = total + jnp.dot(
                R[n, 0:2].reshape(64, 128), Lm[n], preferred_element_type=F32
            )
        CT[...] = 1.0 / (total + 0.001)

    def out_copy(p):
        cols = pl.ds(pl.multiple_of(p * CJ, CJ), CJ)
        return pltpu.make_async_copy(out_v.at[:, cols, :], out.at[:, cols, :], o_sem.at[p])

    def finish(p):
        own = chain_rows[pl.ds(row, 1), :]
        for jp in range(CJ // 2):
            for u in range(2):
                j = 2 * jp + u
                a = acc[p * (CJ // 2) + jp, :, u * 128:(u + 1) * 128]
                a = a * CT[pl.ds(p * CJ + j, 1), :]
                same = own == chain_s[col * 64 + p * CJ + j]
                a = a + jnp.where(same, bT[:, 0:1], bT[:, 1:2])
                T[pl.ds(j, 128, stride=CJ), :] = jnp.transpose(a)
        cols = pl.ds(pl.multiple_of(p * CJ, CJ), CJ)
        out_v[:, cols, :] = (
            T[...].reshape(128, CJ, 128) + pair_v[:, cols, :].astype(F32)
        ).astype(BF16)
        out_copy(p).start()

    def compute(t):
        if t < Q - 1:
            if t > 0:
                lax.fori_loop(0, t, lambda q, _: (unit(q, t), 0)[1], 0)
            lax.fori_loop(0, t + 1, lambda p, _: (unit(t, p), 0)[1], 0)
        else:
            lax.fori_loop(0, t, lambda q, _: (unit(q, t), 0)[1], 0)
            counts()
            p_copy.wait()

            def last(p, _):
                unit(t, p)
                finish(p)
                return 0

            lax.fori_loop(0, Q, last, 0)

    rc(SX, R.at[row, 2:66, pl.ds(pl.multiple_of((1 - core) * 16, 16), 16), :], x_ss, x_rs, sibling).wait_recv()
    side(0)
    first(0)
    side(1)
    for t in range(Q + 2):
        if t + 2 < Q:
            side(t + 2)
        if t + 1 < Q:
            first(t + 1)
        if t < Q:
            partner(t)
        if 1 <= t <= Q:
            second(t - 1)
        if t >= 2:
            third(t - 2)
            fourth(t - 2)
            compute(t - 2)

    for c in sends:
        c.wait_send()
    half_out.wait_send()
    for k in range(8):
        scatter(k, True)
    for p in range(Q):
        out_copy(p).wait()


def per_device(
    homolog_features,
    presence_flags,
    residue_chain_index,
    pair_state,
    standardize_scale,
    standardize_shift,
    left_factor_matrix,
    right_factor_matrix,
    output_weight,
    chain_pair_bias,
):
    anywhere = pl.BlockSpec(memory_space=pl.ANY)
    vmem = pl.BlockSpec(memory_space=pltpu.VMEM)
    smem = pl.BlockSpec(memory_space=pltpu.SMEM)
    dma = pltpu.SemaphoreType.DMA
    return pl.pallas_call(
        kernel,
        out_shape=jax.ShapeDtypeStruct(pair_state.shape, BF16),
        in_specs=[anywhere, vmem, vmem, smem, anywhere, vmem, vmem, vmem, vmem, vmem, vmem],
        out_specs=anywhere,
        scratch_shapes=[
            pltpu.VMEM((8, 8, 128, 256), BF16),
            pltpu.VMEM((512, 128), F32),
            pltpu.VMEM((8, 4, 144, 128), BF16),
            pltpu.VMEM((8, 2, 144, 128), BF16),
            pltpu.VMEM((8, 2, 144, 128), BF16),
            pltpu.VMEM((2, 16, 8, 128, 128), BF16),
            pltpu.VMEM((8, 128, 128), BF16),
            pltpu.VMEM((8, 66, 32, 128), BF16),
            pltpu.VMEM((64, 16, 128), BF16),
            pltpu.VMEM((2048, 128), F32),
            pltpu.VMEM((128, 1024), BF16),
            pltpu.VMEM((64, 256), BF16),
            pltpu.VMEM((32, 128, 256), F32),
            pltpu.VMEM((64, 128), F32),
            pltpu.VMEM((128, 64, 128), BF16),
            pltpu.VMEM((128, 64, 128), BF16),
            pltpu.VMEM((128, 128), F32),
            dma((8,)), dma(()), dma((Q,)),
            dma((8, 4)), dma((8, 2)), dma((8, 2)), dma(()), dma(()),
            dma((Q + 1, 17)), dma((Q + 1, 17)), dma((Q, 9)), dma((Q, 9)),
        ],
        compiler_params=pltpu.CompilerParams(
            collective_id=0, has_side_effects=True, vmem_limit_bytes=60 << 20
        ),
    )(
        homolog_features, presence_flags, residue_chain_index.reshape(8, 128),
        residue_chain_index, pair_state, standardize_scale.reshape(1, -1),
        standardize_shift.reshape(1, -1), left_factor_matrix.T, right_factor_matrix.T,
        output_weight, chain_pair_bias,
    )


def solution(mesh):
    return jax.shard_map(
        per_device,
        mesh=mesh,
        in_specs=(
            P(("row", "col"), None, None),
            P(("row", "col"), None),
            P(),
            P("row", "col", None),
            P(),
            P(),
            P(),
            P(),
            P(),
            P(),
        ),
        out_specs=P("row", "col", None),
        check_vma=False,
    )
```

```python
import jax
import jax.numpy as jnp
from jax import lax
from jax.experimental import pallas as pl
from jax.experimental.pallas import tpu as pltpu
from jax.sharding import PartitionSpec as P

MESH = pl.DeviceIdType.MESH
F32 = jnp.float32
BF16 = jnp.bfloat16
LEFT = ((0, 2), (2, 2), (4, 1), (5, 1), (6, 1), (7, 1))
RIGHT = ((0, 16), (16, 16), (32, 8), (40, 8), (48, 8), (56, 8))
ORDER = (
    "start", "al1out", "prep", "join0", "lS0", "lO0", "turn", "lG0", "halfw", "rS0", "rO0",
    "rO1", "join1", "lO1", "lP0", "lS1", "rG0", "lG1", "rP0", "rS1", "rG1", "lH0", "lO2", "lP1",
    "lS2", "lL0", "rP1", "rH0", "rS2", "rO2", "lG2", "lP2", "lS3", "lZ0", "rP2", "rS3", "lH1",
    "lO3", "rH1", "rO3", "lP3", "lS4", "rP3", "rZ0", "rS4", "u0.2.0.16", "rG2", "lH2", "lO4",
    "lP4", "lS5", "lL1", "rH2", "rO4", "rP4", "rS5", "lG3", "rZ1", "u0.2.16.16", "lZ1", "lL2",
    "rG3", "lH3", "lO5", "lP5", "rP5", "u2.2.0.16", "lZ2", "rH3", "lG4", "rO5", "u2.2.16.16",
    "rZ2", "lH4", "lL3", "rG4", "lG5", "rH4", "lZ3", "u4.2.0.16", "lH5", "u4.2.16.16", "rZ3",
    "lL4", "rH5", "u0.2.32.16", "rG5", "lL5", "u2.2.32.16", "lZ4", "rZ4", "u4.2.32.16", "lZ5",
    "rZ5", "u0.2.48.16", "u2.2.48.16", "u4.2.48.16", "u6.2.0.16", "f0", "u6.2.16.16", "f1",
    "u6.2.32.16", "f2", "u6.2.48.16", "f3",
)
Q = len(LEFT)
MQ = 1
PART = 48
CJ = 16


def kernel(
    feats, flags_h, chain_h, pair, scale_h, shift_h, wl, wr, wout_h, bias_h,
    out,
    F, Y, SL, SR, RL, RR, L, Lm, R, SX, T, WT, PT, acc, CT, SM, pair_v, bT,
    flags, chain, scale, shift, wout, bias,
    f_sem, i_sem, a_ss, a_rl, a_rr, x_ss, x_rs, l_ss, l_rs, r_ss, r_rs,
):
    row = lax.axis_index("row")
    col = lax.axis_index("col")
    yh, x = row // 4, row % 4
    cc, core = col // 2, col % 2
    yl, z = cc // 4, cc % 4

    def dev(yh_, x_, yl_, z_, k_):
        return (yh_ * 4 + x_, yl_ * 8 + z_ * 2 + k_)

    def rc(src, dst, ss, rs, d):
        return pltpu.make_async_remote_copy(
            src_ref=src, dst_ref=dst, send_sem=ss, recv_sem=rs, device_id=d, device_id_type=MESH
        )

    bar = pltpu.get_barrier_semaphore()
    for d in range(1, 16):
        at = lax.rem(row * 2 + core + d, 16)
        pl.semaphore_signal(
            bar, inc=1, device_id=(at // 2, cc * 2 + at % 2), device_id_type=MESH
        )
    for d in range(1, 8):
        for k in range(2):
            pl.semaphore_signal(
                bar, inc=1, device_id=(row, lax.rem(cc + d, 8) * 2 + k), device_id_type=MESH
            )

    def block_of(k):
        return lax.rem(row + cc + k, 8)

    def f_copy(k):
        b = block_of(k)
        return pltpu.make_async_copy(
            feats.at[:, pl.ds(pl.multiple_of(b * 128, 128), 128), :], F.at[k], f_sem.at[k]
        )

    loads = [
        pltpu.make_async_copy(src, dst, i_sem.at[i])
        for i, (src, dst) in enumerate((
            (flags_h, flags), (scale_h, scale), (shift_h, shift),
            (wl, PT.at[0:32]), (wr, PT.at[32:64]),
            (wout_h, wout), (bias_h, bias), (chain_h, chain), (pair, pair_v),
        ))
    ]
    for c in loads[:5]:
        c.start()
    for k in range(8):
        f_copy(k).start()
    for c in loads[5:]:
        c.start()
    for c in loads[:5]:
        c.wait()

    def project(k, _):
        f_copy(k).wait()
        b = block_of(k)
        present = flags[:, pl.ds(pl.multiple_of(b * 128, 128), 128)].astype(F32)
        for sp in range(4):
            v = F[k, 2 * sp:2 * sp + 2].reshape(256, 256).astype(F32)
            mu = jnp.mean(v, axis=-1, keepdims=True)
            d = v - mu
            var = jnp.mean(d * d, axis=-1, keepdims=True)
            nrm = (d * lax.rsqrt(var + 1e-05) * scale[...] + shift[...]).astype(BF16)
            pr = lax.dot_general(
                PT[...], nrm, (((1,), (1,)), ((), ())), preferred_element_type=F32
            )
            for u in range(2):
                s = 2 * sp + u
                Y[pl.ds(s, 64, stride=8), :] = pr[:, u * 128:(u + 1) * 128] * present[s:s + 1, :]
        pad = jnp.concatenate([present, jnp.zeros_like(present)], axis=0).astype(BF16)
        for h in range(2):
            SL[b, h, 0:16, :] = pad
            for g in range(8):
                at = (4 * g + 2 * h) * 8
                SL[b, h, 16 * g + 16:16 * g + 32, :] = Y[at:at + 16, :].astype(BF16)
            SR[b, h, 0:128, :] = Y[256 + h * 128:256 + (h + 1) * 128, :].astype(BF16)
            SR[b, h, 128:144, :] = pad
        return 0

    lax.fori_loop(0, 8, project, 0)

    def left_part(part):
        return slice(0, PART) if part == 0 else slice(PART, 144)

    def left_out(k, h, part):
        b = block_of(k)
        c = rc(
            SL.at[b, h, left_part(part)], RL.at[row, core, left_part(part)],
            a_ss.at[part, k, h], a_rl.at[part, row, core], (b, cc * 2 + h),
        )
        return c, jnp.logical_and(b == row, h == core)

    def right_out(k, h):
        b = block_of(k)
        c = rc(
            SR.at[b, h], RR.at[cc, core], a_ss.at[2, k, h], a_rr.at[cc, core], (row, b * 2 + h)
        )
        return c, jnp.logical_and(b == cc, h == core)

    def every(make, wait):
        def one(k, _):
            for h in range(2):
                c, mine = make(k, h)

                @pl.when(jnp.logical_not(mine))
                def _():
                    c.wait_send() if wait else c.start()

            return 0

        lax.fori_loop(0, 8, one, 0)

    pl.semaphore_wait(bar, 29)

    def start():
        every(lambda k, h: left_out(k, h, 0), False)
        every(right_out, False)
        RL[row, core] = SL[row, core]
        RR[cc, core] = SR[cc, core]

    def prepare():
        for c in loads[5:8]:
            c.wait()
        for g in range(8):
            WT[:, g * 128:(g + 1) * 128] = jnp.transpose(
                wout[g * 128:(g + 1) * 128, :].astype(F32)
            ).astype(BF16)
        bT[...] = jnp.transpose(
            jnp.concatenate([bias[...], jnp.zeros((126, 128), F32)], axis=0)
        )
        T[0:128, :] = jnp.transpose(
            jnp.broadcast_to(chain[pl.ds(cc, 1), :].astype(F32), (128, 128))
        )
        SM[...] = jnp.where(
            T[pl.ds(pl.multiple_of(core * 64, 64), 64), :] == chain[pl.ds(row, 1), :].astype(F32),
            1.0, 0.0,
        )

        def clear(i, _):
            acc[i] = jnp.zeros((128, 256), F32)
            return 0

        lax.fori_loop(0, 32, clear, 0)

    m_own = yl * 4 + z

    def rows_at(m):
        return pl.ds(pl.multiple_of(m * 16, 16), 16)

    def left_in(part):
        for n in range(8):
            for k in range(2):
                @pl.when(jnp.logical_not(jnp.logical_and(n == row, k == core)))
                def _():
                    ref = RL.at[n, k, left_part(part)]
                    rc(ref, ref, a_ss.at[0, 0, 0], a_rl.at[part, n, k], (row, col)).wait_recv()

    def join(n, g):
        a = RL[n, 0, 16 * g + 16:16 * g + 32, :].astype(F32)
        b = RL[n, 1, 16 * g + 16:16 * g + 32, :].astype(F32)
        for u in range(2):
            L[core, 2 * g + u, n, rows_at(m_own), :] = jnp.concatenate(
                [a[8 * u:8 * u + 8], b[8 * u:8 * u + 8]], axis=0
            ).astype(BF16)

    def join_groups(gs):
        def one(n, _):
            for g in gs:
                join(n, g)
            return 0

        lax.fori_loop(0, 8, one, 0)

    e_half = pl.ds(pl.multiple_of(core * 16, 16), 16)
    e_other = pl.ds(pl.multiple_of((1 - core) * 16, 16), 16)
    sibling = dev(yh, x, yl, z, 1 - core)
    half_out = rc(SX, R.at[row, 2:66, e_half, :], x_ss, x_rs, sibling)

    def turn():
        for m in range(8):
            for k in range(2):
                @pl.when(jnp.logical_not(jnp.logical_and(m == cc, k == core)))
                def _():
                    ref = RR.at[m, k]
                    rc(ref, ref, a_ss.at[0, 0, 0], a_rr.at[m, k], (row, col)).wait_recv()
        for ep in range(8):
            parts = [
                RR[m, k, 16 * ep:16 * ep + 16, :].astype(F32) for m in range(8) for k in range(2)
            ]
            for u in range(2):
                T[pl.ds(2 * ep + u, 128, stride=16), :] = jnp.transpose(
                    jnp.concatenate([p[8 * u:8 * u + 8] for p in parts], axis=0)
                )
        SX[...] = (
            T[pl.ds(pl.multiple_of((1 - core) * 1024, 1024), 1024), :]
            .astype(BF16).reshape(64, 16, 128)
        )
        half_out.start()
        R[row, 2:66, e_half, :] = (
            T[pl.ds(pl.multiple_of(core * 1024, 1024), 1024), :].astype(BF16).reshape(64, 16, 128)
        )
        present = jnp.concatenate(
            [RR[m, k, 128:144, :].astype(F32)[0:8] for m in range(8) for k in range(2)], axis=0
        )
        T[0:128, :] = jnp.transpose(present)
        R[row, 0:2] = (
            T[pl.ds(pl.multiple_of(core * 64, 64), 64), :].astype(BF16).reshape(2, 32, 128)
        )

    sends = []

    def l_regions(q, h, m, half):
        lo, num = 2 * LEFT[q][0], 2 * LEFT[q][1]
        n_lo, n_num = h * 4, 4
        if half is not None:
            num //= 2
            lo += half * num
            n_num //= 2
            n_lo = n_lo + half * n_num
        regions = [(q, L.at[h, lo:lo + num, :, rows_at(m), :])]
        if q == MQ:
            regions.append((Q, Lm.at[pl.ds(n_lo, n_num), rows_at(m), :]))
        return regions

    def l_send(q, m, half, to, slot):
        for i, ref in l_regions(q, core, m, half):
            c = rc(ref, ref, l_ss.at[i, slot], l_rs.at[i, slot], to)
            c.start()
            sends.append(c)

    def l_recv(q, h, m, half, slot):
        for i, ref in l_regions(q, h, m, half):
            rc(ref, ref, l_ss.at[i, slot], l_rs.at[i, slot], (row, col)).wait_recv()

    def r_region(p, n, half):
        lo, num = RIGHT[p][0] + 2, RIGHT[p][1]
        if p == 0:
            lo, num = 0, num + 2
        if half is not None:
            num //= 2
            lo += half * num
        return R.at[n, lo:lo + num]

    def r_send(p, n, half, to, slot):
        ref = r_region(p, n, half)
        c = rc(ref, ref, r_ss.at[p, slot], r_rs.at[p, slot], to)
        c.start()
        sends.append(c)

    def r_recv(p, n, half, slot):
        ref = r_region(p, n, half)
        rc(ref, ref, r_ss.at[p, slot], r_rs.at[p, slot], (row, col)).wait_recv()

    zu, zd, zo = lax.rem(z + 1, 4), lax.rem(z + 3, 4), lax.rem(z + 2, 4)
    xu, xd, xo = lax.rem(x + 1, 4), lax.rem(x + 3, 4), lax.rem(x + 2, 4)
    l_up, l_down = dev(yh, x, yl, zu, core), dev(yh, x, yl, zd, core)
    l_side = dev(yh, x, 1 - yl, z, core)
    r_up, r_down = dev(yh, xu, yl, z, core), dev(yh, xd, yl, z, core)
    r_side = dev(1 - yh, x, yl, z, core)
    ys = (yl, 1 - yl)
    hs = (yh, 1 - yh)
    mp, np_ = ys[1] * 4 + z, hs[1] * 4 + x

    def l_side_out(t):
        l_send(t, m_own, None, l_side, 0)

    def r_side_out(t):
        r_send(t, row, None, r_side, 0)

    def l_own(t):
        l_send(t, m_own, None, l_up, 1)
        l_send(t, m_own, None, l_down, 2)
        l_send(t, m_own, None, sibling, 9)

    def r_own(t):
        r_send(t, row, None, r_up, 1)
        r_send(t, row, None, r_down, 2)

    def l_partner(t):
        l_recv(t, core, mp, None, 0)
        l_send(t, mp, None, l_up, 3)
        l_send(t, mp, None, l_down, 4)
        l_send(t, mp, None, sibling, 10)

    def r_partner(t):
        r_recv(t, np_, None, 0)
        r_send(t, np_, None, r_up, 3)
        r_send(t, np_, None, r_down, 4)

    def l_far(t, w):
        lu, ld = ys[w] * 4 + zu, ys[w] * 4 + zd
        l_recv(t, core, ld, None, 1 + 2 * w)
        l_send(t, ld, 0, l_up, 5 + 2 * w)
        l_recv(t, core, lu, None, 2 + 2 * w)
        l_send(t, lu, 1, l_down, 6 + 2 * w)
        l_send(t, ld, None, sibling, 11 + 2 * w)
        l_send(t, lu, None, sibling, 12 + 2 * w)

    def r_far(t, w):
        ru, rd = hs[w] * 4 + xu, hs[w] * 4 + xd
        r_recv(t, rd, None, 1 + 2 * w)
        r_send(t, rd, 0, r_up, 5 + 2 * w)
        r_recv(t, ru, None, 2 + 2 * w)
        r_send(t, ru, 1, r_down, 6 + 2 * w)

    def l_last(t):
        for w in range(2):
            lo = ys[w] * 4 + zo
            l_recv(t, core, lo, 0, 5 + 2 * w)
            l_recv(t, core, lo, 1, 6 + 2 * w)
            l_send(t, lo, None, sibling, 15 + w)

    def r_done(t):
        for w in range(2):
            ro = hs[w] * 4 + xo
            r_recv(t, ro, 0, 5 + 2 * w)
            r_recv(t, ro, 1, 6 + 2 * w)

    def l_done(t):
        for w in range(2):
            l_recv(t, 1 - core, ys[w] * 4 + z, None, 9 + w)
            l_recv(t, 1 - core, ys[w] * 4 + zd, None, 11 + 2 * w)
            l_recv(t, 1 - core, ys[w] * 4 + zu, None, 12 + 2 * w)
            l_recv(t, 1 - core, ys[w] * 4 + zo, None, 15 + w)

    def unit(g0, ng, j0, nj):
        lhs = jnp.concatenate(
            [R[n, pl.ds(2 + j0, nj)].reshape(nj * 32, 128) for n in range(8)], axis=1
        )
        for s0 in range(0, ng, 2):
            sn = min(2, ng - s0)
            prods = []
            for gi in range(sn):
                for h in range(2):
                    rhs = jnp.concatenate(
                        [L[h, (g0 + s0 + gi) * 2 + u].reshape(1024, 128) for u in range(2)], axis=1
                    )
                    prods.append(jnp.dot(lhs, rhs, preferred_element_type=F32).astype(BF16))
            w = WT[:, (g0 + s0) * 128:(g0 + s0 + sn) * 128]
            for jp in range(nj // 2):
                blk = jnp.concatenate(
                    [
                        jnp.concatenate(
                            [
                                o[j * 32:(j + 1) * 32, u * 128:(u + 1) * 128]
                                for o in prods for u in range(2)
                            ],
                            axis=0,
                        )
                        for j in (2 * jp, 2 * jp + 1)
                    ],
                    axis=1,
                )
                acc[j0 // 2 + jp] += jnp.dot(w, blk, preferred_element_type=F32)

    def counts():
        total = jnp.zeros((64, 128), F32)
        for n in range(8):
            total = total + jnp.dot(
                R[n, 0:2].reshape(64, 128), Lm[n], preferred_element_type=F32
            )
        CT[...] = 1.0 / (total + 0.001)

    def finish(p):
        for jp in range(CJ // 2):
            for u in range(2):
                j = 2 * jp + u
                a = acc[p * (CJ // 2) + jp, :, u * 128:(u + 1) * 128]
                a = a * CT[p * CJ + j:p * CJ + j + 1, :]
                same = SM[p * CJ + j:p * CJ + j + 1, :] > 0.5
                a = a + jnp.where(same, bT[:, 0:1], bT[:, 1:2])
                T[pl.ds(j, 128, stride=CJ), :] = jnp.transpose(a)
        cols = slice(p * CJ, (p + 1) * CJ)
        out[:, cols, :] = (
            T[...].reshape(128, CJ, 128) + pair_v[:, cols, :].astype(F32)
        ).astype(BF16)

    def join_first():
        left_in(0)
        join_groups((0, 1))
        for i in range(4):
            n = core * 4 + i
            a = RL[n, 0, 0:16, :].astype(F32)
            b = RL[n, 1, 0:16, :].astype(F32)
            Lm[n, rows_at(m_own), :] = jnp.concatenate([a[0:8], b[0:8]], axis=0).astype(BF16)

    def join_rest():
        left_in(1)
        join_groups((2, 3, 4, 5, 6, 7))

    def half_in():
        rc(SX, R.at[row, 2:66, e_other, :], x_ss, x_rs, sibling).wait_recv()

    def finish_from(p):
        if not finished:
            counts()
            loads[8].wait()
        finished.append(p)
        finish(p)

    finished = []
    once = {
        "start": start, "prep": prepare, "join0": join_first, "join1": join_rest,
        "turn": turn, "halfw": half_in,
        "al1out": lambda: every(lambda k, h: left_out(k, h, 1), False),
    }
    steps = {
        "lS": l_side_out, "lO": l_own, "lP": l_partner, "lL": l_last, "lZ": l_done,
        "lG": lambda t: l_far(t, 0), "lH": lambda t: l_far(t, 1),
        "rS": r_side_out, "rO": r_own, "rP": r_partner, "rZ": r_done,
        "rG": lambda t: r_far(t, 0), "rH": lambda t: r_far(t, 1),
    }
    for name in ORDER:
        if name in once:
            once[name]()
        elif name[0] == "u":
            unit(*[int(v) for v in name[1:].split(".")])
        elif name[0] == "f":
            finish_from(int(name[1:]))
        else:
            steps[name[:2]](int(name[2:]))

    for c in sends:
        c.wait_send()
    half_out.wait_send()
    every(lambda k, h: left_out(k, h, 0), True)
    every(right_out, True)
    every(lambda k, h: left_out(k, h, 1), True)


def per_device(
    homolog_features,
    presence_flags,
    residue_chain_index,
    pair_state,
    standardize_scale,
    standardize_shift,
    left_factor_matrix,
    right_factor_matrix,
    output_weight,
    chain_pair_bias,
):
    anywhere = pl.BlockSpec(memory_space=pl.ANY)
    dma = pltpu.SemaphoreType.DMA
    return pl.pallas_call(
        kernel,
        out_shape=pltpu.VMEM(pair_state.shape, BF16),
        in_specs=[anywhere] * 10,
        out_specs=pl.BlockSpec(memory_space=pltpu.VMEM),
        scratch_shapes=[
            pltpu.VMEM((8, 8, 128, 256), BF16),
            pltpu.VMEM((512, 128), F32),
            pltpu.VMEM((8, 2, 144, 128), BF16),
            pltpu.VMEM((8, 2, 144, 128), BF16),
            pltpu.VMEM((8, 2, 144, 128), BF16),
            pltpu.VMEM((8, 2, 144, 128), BF16),
            pltpu.VMEM((2, 16, 8, 128, 128), BF16),
            pltpu.VMEM((8, 128, 128), BF16),
            pltpu.VMEM((8, 66, 32, 128), BF16),
            pltpu.VMEM((64, 16, 128), BF16),
            pltpu.VMEM((2048, 128), F32),
            pltpu.VMEM((128, 1024), BF16),
            pltpu.VMEM((64, 256), BF16),
            pltpu.VMEM((32, 128, 256), F32),
            pltpu.VMEM((64, 128), F32),
            pltpu.VMEM((64, 128), F32),
            pltpu.VMEM((128, 64, 128), BF16),
            pltpu.VMEM((128, 128), F32),
            pltpu.VMEM((8, 1024), jnp.int32),
            pltpu.VMEM((8, 128), jnp.int32),
            pltpu.VMEM((1, 256), F32),
            pltpu.VMEM((1, 256), F32),
            pltpu.VMEM((1024, 128), BF16),
            pltpu.VMEM((2, 128), F32),
            dma((8,)), dma((9,)),
            dma((3, 8, 2)), dma((2, 8, 2)), dma((8, 2)), dma(()), dma(()),
            dma((Q + 1, 17)), dma((Q + 1, 17)), dma((Q, 9)), dma((Q, 9)),
        ],
        compiler_params=pltpu.CompilerParams(
            collective_id=0, has_side_effects=True, vmem_limit_bytes=61 << 20
        ),
    )(
        homolog_features, presence_flags, residue_chain_index.reshape(8, 128),
        pair_state, standardize_scale.reshape(1, -1),
        standardize_shift.reshape(1, -1), left_factor_matrix.T, right_factor_matrix.T,
        output_weight, chain_pair_bias,
    )


def solution(mesh):
    return jax.shard_map(
        per_device,
        mesh=mesh,
        in_specs=(
            P(("row", "col"), None, None),
            P(("row", "col"), None),
            P(),
            P("row", "col", None),
            P(),
            P(),
            P(),
            P(),
            P(),
            P(),
        ),
        out_specs=P("row", "col", None),
        check_vma=False,
    )
```

```python
import jax
import jax.numpy as jnp
from jax import lax
from jax.experimental import pallas as pl
from jax.experimental.pallas import tpu as pltpu
from jax.sharding import PartitionSpec as Spec

MESH = pl.DeviceIdType.MESH
F32 = jnp.float32
BF16 = jnp.bfloat16
LEFT = ((0, 2), (2, 2), (4, 2), (6, 1), (7, 1))
RIGHT = ((0, 16), (16, 16), (32, 16), (48, 8), (56, 8))
ORDER = (
    "start", "prep", "al1out", "join0", "lO0", "lS0", "turn", "rO0", "lR0", "lP0", "rS0", "rO1",
    "join1", "lS1", "lO2", "lB0", "lH0", "lO1", "rG0", "rS1", "rP0", "lR1", "lG0", "lS2", "rG1",
    "rS2", "lP1", "lO3", "rP1", "rO2", "lR2", "lL0", "lB1", "rH0", "lP2", "lZ0", "lH1", "rP2",
    "rH1", "lG1", "lB2", "rG2", "rS3", "lH2", "lS4", "lS3", "rZ0", "u0.2.0.16", "rP3", "lL1",
    "rS4", "rH2", "lR4", "rO4", "rO3", "lP4", "lR3", "lG2", "lP3", "lO4", "rZ1", "u0.2.16.16",
    "lZ1", "u2.2.0.16", "rP4", "lB4", "u2.2.16.16", "lL2", "rH3", "lB3", "lH4", "rZ2",
    "u0.2.32.16", "lH3", "u2.2.32.16", "rG4", "lG4", "rG3", "lZ2", "u4.2.16.16", "lG3", "rH4",
    "u4.2.32.16", "u4.2.0.16", "lL4", "rZ3", "lL3", "rZ4", "u4.2.48.16", "u2.2.48.16", "lZ4",
    "u0.2.48.16", "lZ3", "u6.2.16.16", "f1", "u6.2.0.16", "f0", "u6.2.48.16", "f3",
    "u6.2.32.16", "f2",
)
Q, P = len(LEFT), len(RIGHT)
MQ = 1
PART = 48
CJ = 16


def kernel(
    feats, flags_h, chain_h, pair, scale_h, shift_h, wl, wr, wout_h, bias_h,
    out,
    F, Y, SL, SR, RL, RR, L, Lm, LX, LXm, R, T, WT, PT, acc, CT, SM, pair_v, bT,
    flags, chain, scale, shift, wout, bias,
    f_sem, i_sem, a_ss, a_rl, a_rr, l_ss, l_rs, r_ss, r_rs,
):
    row = lax.axis_index("row")
    col = lax.axis_index("col")
    yh, x = row // 4, row % 4
    cc, core = col // 2, col % 2
    yl, z = cc // 4, cc % 4

    def dev(yh_, x_, yl_, z_, k_):
        return (yh_ * 4 + x_, yl_ * 8 + z_ * 2 + k_)

    def rc(src, dst, ss, rs, d):
        return pltpu.make_async_remote_copy(
            src_ref=src, dst_ref=dst, send_sem=ss, recv_sem=rs, device_id=d, device_id_type=MESH
        )

    bar = pltpu.get_barrier_semaphore()
    greeted = [(row, lax.rem(col + d, 16)) for d in range(1, 16)]
    greeted += [
        (yh * 4 + lax.rem(x + d, 4), cc * 2 + k) for d in range(1, 4) for k in range(2)
    ]
    greeted += [dev(1 - yh, x, yl, z, core), dev(1 - yh, x, 1 - yl, z, core)]
    for d in greeted:
        pl.semaphore_signal(bar, inc=1, device_id=d, device_id_type=MESH)

    def block_of(k):
        return lax.rem(row + cc + k, 8)

    def f_copy(k):
        b = block_of(k)
        return pltpu.make_async_copy(
            feats.at[:, pl.ds(pl.multiple_of(b * 128, 128), 128), :], F.at[k], f_sem.at[k]
        )

    loads = [
        pltpu.make_async_copy(src, dst, i_sem.at[i])
        for i, (src, dst) in enumerate((
            (flags_h, flags), (scale_h, scale), (shift_h, shift),
            (wl, PT.at[0:32]), (wr, PT.at[32:64]),
            (wout_h, wout), (bias_h, bias), (chain_h, chain), (pair, pair_v),
        ))
    ]
    for c in loads[:5]:
        c.start()
    for k in range(8):
        f_copy(k).start()
    for c in loads[5:]:
        c.start()
    for c in loads[:5]:
        c.wait()

    def project(k, _):
        f_copy(k).wait()
        b = block_of(k)
        present = flags[:, pl.ds(pl.multiple_of(b * 128, 128), 128)].astype(F32)
        for sp in range(4):
            v = F[k, 2 * sp:2 * sp + 2].reshape(256, 256).astype(F32)
            mu = jnp.mean(v, axis=-1, keepdims=True)
            d = v - mu
            var = jnp.mean(d * d, axis=-1, keepdims=True)
            nrm = (d * lax.rsqrt(var + 1e-05) * scale[...] + shift[...]).astype(BF16)
            pr = lax.dot_general(
                PT[...], nrm, (((1,), (1,)), ((), ())), preferred_element_type=F32
            )
            for u in range(2):
                s = 2 * sp + u
                Y[pl.ds(s, 64, stride=8), :] = pr[:, u * 128:(u + 1) * 128] * present[s:s + 1, :]
        pad = jnp.concatenate([present, jnp.zeros_like(present)], axis=0).astype(BF16)
        for h in range(2):
            SL[b, h, 0:16, :] = pad
            for g in range(8):
                at = (4 * g + 2 * h) * 8
                SL[b, h, 16 * g + 16:16 * g + 32, :] = Y[at:at + 16, :].astype(BF16)
        low = lax.broadcasted_iota(jnp.int32, (16, 128), 1) < 64
        for g in range(8):
            y = Y[256 + 32 * g:288 + 32 * g, :]
            e0 = jnp.concatenate([y[0:8], y[16:24]], axis=0)
            e1 = jnp.concatenate([y[8:16], y[24:32]], axis=0)
            at = slice(16 * g, 16 * g + 16)
            SR[b, 0, at, :] = jnp.where(low, e0, pltpu.roll(e1, 64, 1)).astype(BF16)
            SR[b, 1, at, :] = jnp.where(low, pltpu.roll(e0, 64, 1), e1).astype(BF16)
        both = jnp.concatenate([present, jnp.zeros_like(present)], axis=0)
        SR[b, 0, 128:144, :] = pad
        SR[b, 1, 128:144, :] = pltpu.roll(both, 64, 1).astype(BF16)
        return 0

    lax.fori_loop(0, 8, project, 0)

    def left_part(part):
        return slice(0, PART) if part == 0 else slice(PART, 144)

    def left_out(k, h, part):
        b = block_of(k)
        c = rc(
            SL.at[b, h, left_part(part)], RL.at[b // 4, x, core, left_part(part)],
            a_ss.at[part, k, h], a_rl.at[part, b // 4, x, core],
            (yh * 4 + lax.rem(b, 4), cc * 2 + h),
        )
        return c, jnp.logical_and(lax.rem(b, 4) == x, h == core)

    def right_out(k, h):
        b = block_of(k)
        c = rc(
            SR.at[b, h], RR.at[cc, core], a_ss.at[2, k, h], a_rr.at[cc, core], (row, b * 2 + h)
        )
        return c, jnp.logical_and(b == cc, h == core)

    def every(make, wait):
        def one(k, _):
            for h in range(2):
                c, mine = make(k, h)

                @pl.when(jnp.logical_not(mine))
                def _():
                    c.wait_send() if wait else c.start()

            return 0

        lax.fori_loop(0, 8, one, 0)

    pl.semaphore_wait(bar, len(greeted))

    def start():
        every(lambda k, h: left_out(k, h, 0), False)
        every(right_out, False)
        for i in range(2):
            RL[i, x, core] = SL[i * 4 + x, core]
        RR[cc, core] = SR[cc, core]

    def prepare():
        for c in loads[5:8]:
            c.wait()
        for g in range(8):
            WT[:, g * 128:(g + 1) * 128] = jnp.transpose(
                wout[g * 128:(g + 1) * 128, :].astype(F32)
            ).astype(BF16)
        bT[...] = jnp.transpose(
            jnp.concatenate([bias[...], jnp.zeros((126, 128), F32)], axis=0)
        )
        T[0:128, :] = jnp.transpose(
            jnp.broadcast_to(chain[pl.ds(cc, 1), :].astype(F32), (128, 128))
        )
        SM[...] = jnp.where(
            T[pl.ds(pl.multiple_of(core * 64, 64), 64), :] == chain[pl.ds(row, 1), :].astype(F32),
            1.0, 0.0,
        )

        def clear(i, _):
            acc[i] = jnp.zeros((128, 256), F32)
            return 0

        lax.fori_loop(0, 32, clear, 0)

    m_own = yl * 4 + z

    def rows_at(m):
        return pl.ds(pl.multiple_of(m * 16, 16), 16)

    def left_in(part):
        for i in range(2):
            for n in range(4):
                for k in range(2):
                    @pl.when(jnp.logical_not(jnp.logical_and(n == x, k == core)))
                    def _():
                        ref = RL.at[i, n, k, left_part(part)]
                        rc(ref, ref, a_ss.at[0, 0, 0], a_rl.at[part, i, n, k], (row, col)).wait_recv()

    def joined(i, n, at):
        a = RL[i, n, 0, at:at + 16, :].astype(F32)
        b = RL[i, n, 1, at:at + 16, :].astype(F32)
        return [
            jnp.concatenate([a[8 * u:8 * u + 8], b[8 * u:8 * u + 8]], axis=0).astype(BF16)
            for u in range(2)
        ]

    def join_groups(gs):
        def one(n, _):
            for g in gs:
                for u, v in enumerate(joined(yh, n, 16 * g + 16)):
                    L[core, 2 * g + u, yh * 4 + n, rows_at(m_own), :] = v
                for u, v in enumerate(joined(1 - yh, n, 16 * g + 16)):
                    LX[2 * g + u, n] = v
            return 0

        lax.fori_loop(0, 4, one, 0)

    sibling = dev(yh, x, yl, z, 1 - core)

    def turn():
        for m in range(8):
            for k in range(2):
                @pl.when(jnp.logical_not(jnp.logical_and(m == cc, k == core)))
                def _():
                    ref = RR.at[m, k]
                    rc(ref, ref, a_ss.at[0, 0, 0], a_rr.at[m, k], (row, col)).wait_recv()
        for g in range(8):
            parts = [
                RR[m, k, 16 * g:16 * g + 16, :].astype(F32) for m in range(8) for k in range(2)
            ]
            for u in range(2):
                t = jnp.transpose(
                    jnp.concatenate([p[8 * u:8 * u + 8] for p in parts], axis=0)
                )
                for i in range(2):
                    T[pl.ds(4 * g + 2 * u + i, 64, stride=32), :] = t[64 * i:64 * i + 64]
        R[row, 2:66] = T[...].astype(BF16).reshape(64, 32, 128)
        t = jnp.transpose(jnp.concatenate(
            [RR[m, k, 128:144, :].astype(F32)[0:8] for m in range(8) for k in range(2)], axis=0
        ))
        R[row, 0:2] = t[0:64].astype(BF16).reshape(2, 32, 128)

    sends = []

    ALL = slice(None)

    def l_regions(q, h, m, part=None, yhalf=None):
        lo, num = 2 * LEFT[q][0], 2 * LEFT[q][1]
        if part is not None:
            num //= 2
            lo += part * num
        n = ALL if yhalf is None else pl.ds(yhalf * 4, 4)
        regions = [(q, L.at[h, lo:lo + num, n, rows_at(m), :])]
        if q == MQ:
            i = part if part is not None else ALL if yhalf is None else yhalf
            regions.append((Q, Lm.at[i, pl.ds(h * 2, 2), rows_at(m), :]))
        return regions

    def l_send(q, m, to, slot, **which):
        for i, ref in l_regions(q, core, m, **which):
            c = rc(ref, ref, l_ss.at[i, slot], l_rs.at[i, slot], to)
            c.start()
            sends.append(c)

    def l_recv(q, h, m, slot, **which):
        for i, ref in l_regions(q, h, m, **which):
            rc(ref, ref, l_ss.at[i, slot], l_rs.at[i, slot], (row, col)).wait_recv()

    def r_region(p, n, half):
        lo, num = RIGHT[p][0] + 2, RIGHT[p][1]
        if p == 0:
            lo, num = 0, num + 2
        if half is not None:
            num //= 2
            lo += half * num
        return R.at[n, lo:lo + num]

    def r_send(p, n, half, to, slot):
        ref = r_region(p, n, half)
        c = rc(ref, ref, r_ss.at[p, slot], r_rs.at[p, slot], to)
        c.start()
        sends.append(c)

    def r_recv(p, n, half, slot):
        ref = r_region(p, n, half)
        rc(ref, ref, r_ss.at[p, slot], r_rs.at[p, slot], (row, col)).wait_recv()

    zu, zd, zo = lax.rem(z + 1, 4), lax.rem(z + 3, 4), lax.rem(z + 2, 4)
    xu, xd, xo = lax.rem(x + 1, 4), lax.rem(x + 3, 4), lax.rem(x + 2, 4)
    l_up, l_down = dev(yh, x, yl, zu, core), dev(yh, x, yl, zd, core)
    l_side = dev(yh, x, 1 - yl, z, core)
    l_cross = dev(1 - yh, x, 1 - yl, z, core)
    r_up, r_down = dev(yh, xu, yl, z, core), dev(yh, xd, yl, z, core)
    r_side = dev(1 - yh, x, yl, z, core)
    ys = (yl, 1 - yl)
    hs = (yh, 1 - yh)
    mp, np_ = ys[1] * 4 + z, hs[1] * 4 + x

    def l_side_out(t):
        l_send(t, m_own, l_side, 0, yhalf=yh)
        lo, num = 2 * LEFT[t][0], 2 * LEFT[t][1]
        away = [LX.at[lo:lo + num], LXm.at[pl.ds(core * 2, 2)]]
        for src, (i, dst) in zip(away, l_regions(t, core, m_own, yhalf=yh)):
            c = rc(src, dst, l_ss.at[i, 17], l_rs.at[i, 17], l_cross)
            c.start()
            sends.append(c)

    def l_pass(t):
        l_recv(t, core, mp, 17, yhalf=1 - yh)
        l_send(t, mp, l_side, 18, yhalf=1 - yh)

    def r_side_out(t):
        r_send(t, row, None, r_side, 0)

    def l_own(t):
        l_send(t, m_own, l_up, 1, yhalf=yh)
        l_send(t, m_own, l_down, 2, yhalf=yh)
        l_send(t, m_own, sibling, 9, yhalf=yh)

    def l_own_rest(t):
        l_recv(t, core, m_own, 18, yhalf=1 - yh)
        l_send(t, m_own, l_up, 19, yhalf=1 - yh)
        l_send(t, m_own, l_down, 20, yhalf=1 - yh)
        l_send(t, m_own, sibling, 21, yhalf=1 - yh)

    def r_own(t):
        r_send(t, row, None, r_up, 1)
        r_send(t, row, None, r_down, 2)

    def l_partner(t):
        l_recv(t, core, mp, 0, yhalf=yh)
        l_send(t, mp, l_up, 3)
        l_send(t, mp, l_down, 4)
        l_send(t, mp, sibling, 10)

    def r_partner(t):
        r_recv(t, np_, None, 0)
        r_send(t, np_, None, r_up, 3)
        r_send(t, np_, None, r_down, 4)

    def l_near(t, m, slot, rest, w):
        if w:
            l_recv(t, core, m, slot + 2)
        else:
            l_recv(t, core, m, slot, yhalf=yh)
            l_recv(t, core, m, rest, yhalf=1 - yh)

    def l_far(t, w):
        lu, ld = ys[w] * 4 + zu, ys[w] * 4 + zd
        l_near(t, ld, 1, 19, w)
        l_send(t, ld, l_up, 5 + 2 * w, part=0)
        l_near(t, lu, 2, 20, w)
        l_send(t, lu, l_down, 6 + 2 * w, part=1)
        l_send(t, ld, sibling, 11 + 2 * w)
        l_send(t, lu, sibling, 12 + 2 * w)

    def r_far(t, w):
        ru, rd = hs[w] * 4 + xu, hs[w] * 4 + xd
        r_recv(t, rd, None, 1 + 2 * w)
        r_send(t, rd, 0, r_up, 5 + 2 * w)
        r_recv(t, ru, None, 2 + 2 * w)
        r_send(t, ru, 1, r_down, 6 + 2 * w)

    def l_last(t):
        for w in range(2):
            lo = ys[w] * 4 + zo
            l_recv(t, core, lo, 5 + 2 * w, part=0)
            l_recv(t, core, lo, 6 + 2 * w, part=1)
            l_send(t, lo, sibling, 15 + w)

    def r_done(t):
        for w in range(2):
            ro = hs[w] * 4 + xo
            r_recv(t, ro, 0, 5 + 2 * w)
            r_recv(t, ro, 1, 6 + 2 * w)

    def l_done(t):
        l_recv(t, 1 - core, m_own, 9, yhalf=yh)
        l_recv(t, 1 - core, m_own, 21, yhalf=1 - yh)
        l_recv(t, 1 - core, mp, 10)
        for w in range(2):
            l_recv(t, 1 - core, ys[w] * 4 + zd, 11 + 2 * w)
            l_recv(t, 1 - core, ys[w] * 4 + zu, 12 + 2 * w)
            l_recv(t, 1 - core, ys[w] * 4 + zo, 15 + w)

    def unit(g0, ng, j0, nj):
        lhs = jnp.concatenate(
            [R[n, pl.ds(2 + j0, nj)].reshape(nj * 32, 128) for n in range(8)], axis=1
        )
        for s0 in range(0, ng, 2):
            sn = min(2, ng - s0)
            prods = []
            for gi in range(sn):
                for h in range(2):
                    rhs = jnp.concatenate(
                        [L[h, (g0 + s0 + gi) * 2 + u].reshape(1024, 128) for u in range(2)], axis=1
                    )
                    prods.append(jnp.dot(lhs, rhs, preferred_element_type=F32).astype(BF16))
            w = WT[:, (g0 + s0) * 128:(g0 + s0 + sn) * 128]
            for jp in range(nj // 2):
                blk = jnp.concatenate(
                    [
                        jnp.concatenate(
                            [
                                o[j * 32:(j + 1) * 32, u * 128:(u + 1) * 128]
                                for o in prods for u in range(2)
                            ],
                            axis=0,
                        )
                        for j in (2 * jp, 2 * jp + 1)
                    ],
                    axis=1,
                )
                acc[j0 // 2 + jp] += jnp.dot(w, blk, preferred_element_type=F32)

    def counts():
        total = jnp.zeros((64, 128), F32)
        for n in range(8):
            total = total + jnp.dot(
                R[n, 0:2].reshape(64, 128), Lm[n // 4, n % 4], preferred_element_type=F32
            )
        CT[...] = 1.0 / (total + 0.001)

    def finish(p):
        for jp in range(CJ // 2):
            for u in range(2):
                j = 2 * jp + u
                a = acc[p * (CJ // 2) + jp, :, u * 128:(u + 1) * 128]
                a = a * CT[p * CJ + j:p * CJ + j + 1, :]
                same = SM[p * CJ + j:p * CJ + j + 1, :] > 0.5
                a = a + jnp.where(same, bT[:, 0:1], bT[:, 1:2])
                T[pl.ds(j, 128, stride=CJ), :] = jnp.transpose(a)
        cols = slice(p * CJ, (p + 1) * CJ)
        out[:, cols, :] = (
            T[...].reshape(128, CJ, 128) + pair_v[:, cols, :].astype(F32)
        ).astype(BF16)

    def join_first():
        left_in(0)
        join_groups((0, 1))
        for i in range(2):
            n = core * 2 + i
            Lm[yh, n, rows_at(m_own), :] = joined(yh, n, 0)[0]
            LXm[n] = joined(1 - yh, n, 0)[0]

    def join_rest():
        left_in(1)
        join_groups((2, 3, 4, 5, 6, 7))

    def finish_from(p):
        if not finished:
            counts()
            loads[8].wait()
        finished.append(p)
        finish(p)

    finished = []
    once = {
        "start": start, "prep": prepare, "join0": join_first, "join1": join_rest,
        "turn": turn,
        "al1out": lambda: every(lambda k, h: left_out(k, h, 1), False),
    }
    steps = {
        "lS": l_side_out, "lR": l_pass, "lO": l_own, "lP": l_partner, "lB": l_own_rest,
        "lL": l_last, "lZ": l_done,
        "lG": lambda t: l_far(t, 0), "lH": lambda t: l_far(t, 1),
        "rS": r_side_out, "rO": r_own, "rP": r_partner, "rZ": r_done,
        "rG": lambda t: r_far(t, 0), "rH": lambda t: r_far(t, 1),
    }
    for name in ORDER:
        if name in once:
            once[name]()
        elif name[0] == "u":
            unit(*[int(v) for v in name[1:].split(".")])
        elif name[0] == "f":
            finish_from(int(name[1:]))
        else:
            steps[name[:2]](int(name[2:]))

    for c in sends:
        c.wait_send()
    every(lambda k, h: left_out(k, h, 0), True)
    every(right_out, True)
    every(lambda k, h: left_out(k, h, 1), True)


def per_device(
    homolog_features,
    presence_flags,
    residue_chain_index,
    pair_state,
    standardize_scale,
    standardize_shift,
    left_factor_matrix,
    right_factor_matrix,
    output_weight,
    chain_pair_bias,
):
    anywhere = pl.BlockSpec(memory_space=pl.ANY)
    dma = pltpu.SemaphoreType.DMA
    return pl.pallas_call(
        kernel,
        out_shape=pltpu.VMEM(pair_state.shape, BF16),
        in_specs=[anywhere] * 10,
        out_specs=pl.BlockSpec(memory_space=pltpu.VMEM),
        scratch_shapes=[
            pltpu.VMEM((8, 8, 128, 256), BF16),
            pltpu.VMEM((512, 128), F32),
            pltpu.VMEM((8, 2, 144, 128), BF16),
            pltpu.VMEM((8, 2, 144, 128), BF16),
            pltpu.VMEM((2, 4, 2, 144, 128), BF16),
            pltpu.VMEM((8, 2, 144, 128), BF16),
            pltpu.VMEM((2, 16, 8, 128, 128), BF16),
            pltpu.VMEM((2, 4, 128, 128), BF16),
            pltpu.VMEM((16, 4, 16, 128), BF16),
            pltpu.VMEM((4, 16, 128), BF16),
            pltpu.VMEM((8, 66, 32, 128), BF16),
            pltpu.VMEM((2048, 128), F32),
            pltpu.VMEM((128, 1024), BF16),
            pltpu.VMEM((64, 256), BF16),
            pltpu.VMEM((32, 128, 256), F32),
            pltpu.VMEM((64, 128), F32),
            pltpu.VMEM((64, 128), F32),
            pltpu.VMEM((128, 64, 128), BF16),
            pltpu.VMEM((128, 128), F32),
            pltpu.VMEM((8, 1024), jnp.int32),
            pltpu.VMEM((8, 128), jnp.int32),
            pltpu.VMEM((1, 256), F32),
            pltpu.VMEM((1, 256), F32),
            pltpu.VMEM((1024, 128), BF16),
            pltpu.VMEM((2, 128), F32),
            dma((8,)), dma((9,)),
            dma((3, 8, 2)), dma((2, 2, 4, 2)), dma((8, 2)),
            dma((Q + 1, 22)), dma((Q + 1, 22)), dma((P, 9)), dma((P, 9)),
        ],
        compiler_params=pltpu.CompilerParams(
            collective_id=0, has_side_effects=True, vmem_limit_bytes=61 << 20
        ),
    )(
        homolog_features, presence_flags, residue_chain_index.reshape(8, 128),
        pair_state, standardize_scale.reshape(1, -1),
        standardize_shift.reshape(1, -1), left_factor_matrix.T, right_factor_matrix.T,
        output_weight, chain_pair_bias,
    )


def solution(mesh):
    return jax.shard_map(
        per_device,
        mesh=mesh,
        in_specs=(
            Spec(("row", "col"), None, None),
            Spec(("row", "col"), None),
            Spec(),
            Spec("row", "col", None),
            Spec(),
            Spec(),
            Spec(),
            Spec(),
            Spec(),
            Spec(),
        ),
        out_specs=Spec("row", "col", None),
        check_vma=False,
    )
```

```python
import jax
import jax.numpy as jnp
from jax import lax
from jax.experimental import pallas as pl
from jax.experimental.pallas import tpu as pltpu
from jax.sharding import PartitionSpec as Spec

MESH = pl.DeviceIdType.MESH
F32 = jnp.float32
BF16 = jnp.bfloat16
LEFT = ((0, 2), (2, 2), (4, 2), (6, 1), (7, 1))
RIGHT = ((0, 16), (16, 16), (32, 16), (48, 8), (56, 8))
ORDER = (
    "start", "prep", "al1out", "join0", "lO0", "lS0", "turn", "rO0", "lR0", "lP0", "rS0", "rO1",
    "join1", "lS1", "lO2", "lB0", "lH0", "lO1", "rG0", "rS1", "rP0", "lR1", "lG0", "lS2", "rG1",
    "rS2", "lP1", "lO3", "rP1", "rO2", "lR2", "lL0", "lB1", "rH0", "lP2", "lZ0", "lH1", "rP2",
    "rH1", "lG1", "lB2", "rG2", "rS3", "lH2", "lS4", "lS3", "rZ0", "u0.2.0.16", "rP3", "lL1",
    "rS4", "rH2", "lR4", "rO4", "rO3", "lP4", "lR3", "lG2", "lP3", "lO4", "rZ1", "u0.2.16.16",
    "lZ1", "u2.2.0.16", "rP4", "lB4", "u2.2.16.16", "lL2", "rH3", "lB3", "lH4", "rZ2",
    "u0.2.32.16", "lH3", "u2.2.32.16", "rG4", "lG4", "rG3", "lZ2", "u4.2.16.16", "lG3", "rH4",
    "u4.2.32.16", "u4.2.0.16", "lL4", "rZ3", "lL3", "rZ4", "u4.2.48.16", "u2.2.48.16", "lZ4",
    "u0.2.48.16", "lZ3", "u6.2.16.16", "f1", "u6.2.0.16", "f0", "u6.2.48.16", "f3",
    "u6.2.32.16", "f2",
)
Q, P = len(LEFT), len(RIGHT)
MQ = 1
PART = 48
CJ = 16


def kernel(
    feats, flags_h, chain_h, pair, scale_h, shift_h, wl, wr, wout_h, bias_h,
    out,
    F, Y, SL, SR, RL, RR, L, Lm, LX, LXm, R, T, WT, PT, acc, CT, SM, pair_v, bT,
    flags, chain, scale, shift, wout, bias,
    f_sem, i_sem, a_ss, a_rl, a_rr, l_ss, l_rs, r_ss, r_rs,
):
    row = lax.axis_index("row")
    col = lax.axis_index("col")
    yh, x = row // 4, row % 4
    cc, core = col // 2, col % 2
    yl, z = cc // 4, cc % 4

    def dev(yh_, x_, yl_, z_, k_):
        return (yh_ * 4 + x_, yl_ * 8 + z_ * 2 + k_)

    def rc(src, dst, ss, rs, d):
        return pltpu.make_async_remote_copy(
            src_ref=src, dst_ref=dst, send_sem=ss, recv_sem=rs, device_id=d, device_id_type=MESH
        )

    bar = pltpu.get_barrier_semaphore()
    greeted = [(row, lax.rem(col + d, 16)) for d in range(1, 16)]
    greeted += [
        (yh * 4 + lax.rem(x + d, 4), cc * 2 + k) for d in range(1, 4) for k in range(2)
    ]
    greeted += [dev(1 - yh, x, yl, z, core), dev(1 - yh, x, 1 - yl, z, core)]
    for d in greeted:
        pl.semaphore_signal(bar, inc=1, device_id=d, device_id_type=MESH)

    def block_of(k):
        return lax.rem(row + cc + k, 8)

    def f_copy(k):
        b = block_of(k)
        return pltpu.make_async_copy(
            feats.at[:, pl.ds(pl.multiple_of(b * 128, 128), 128), :], F.at[k], f_sem.at[k]
        )

    loads = [
        pltpu.make_async_copy(src, dst, i_sem.at[i])
        for i, (src, dst) in enumerate((
            (flags_h, flags), (scale_h, scale), (shift_h, shift),
            (wl, PT.at[0:32]), (wr, PT.at[32:64]),
            (wout_h, wout), (bias_h, bias), (chain_h, chain), (pair, pair_v),
        ))
    ]
    for c in loads[:5]:
        c.start()
    for k in range(8):
        f_copy(k).start()
    for c in loads[5:]:
        c.start()
    for c in loads[:5]:
        c.wait()

    def project(k):
        f_copy(k).wait()
        b = block_of(k)
        present = flags[:, pl.ds(pl.multiple_of(b * 128, 128), 128)].astype(F32)
        for sp in range(4):
            v = F[k, 2 * sp:2 * sp + 2].reshape(256, 256).astype(F32)
            mu = jnp.mean(v, axis=-1, keepdims=True)
            d = v - mu
            var = jnp.mean(d * d, axis=-1, keepdims=True)
            nrm = (d * lax.rsqrt(var + 1e-05) * scale[...] + shift[...]).astype(BF16)
            pr = lax.dot_general(
                PT[...], nrm, (((1,), (1,)), ((), ())), preferred_element_type=F32
            )
            for u in range(2):
                s = 2 * sp + u
                Y[pl.ds(s, 64, stride=8), :] = pr[:, u * 128:(u + 1) * 128] * present[s:s + 1, :]
        pad = jnp.concatenate([present, jnp.zeros_like(present)], axis=0).astype(BF16)
        for h in range(2):
            SL[b, h, 0:16, :] = pad
            for g in range(8):
                at = (4 * g + 2 * h) * 8
                SL[b, h, 16 * g + 16:16 * g + 32, :] = Y[at:at + 16, :].astype(BF16)
        low = lax.broadcasted_iota(jnp.int32, (16, 128), 1) < 64
        for g in range(8):
            y = Y[256 + 32 * g:288 + 32 * g, :]
            e0 = jnp.concatenate([y[0:8], y[16:24]], axis=0)
            e1 = jnp.concatenate([y[8:16], y[24:32]], axis=0)
            at = slice(16 * g, 16 * g + 16)
            SR[b, 0, at, :] = jnp.where(low, e0, pltpu.roll(e1, 64, 1)).astype(BF16)
            SR[b, 1, at, :] = jnp.where(low, pltpu.roll(e0, 64, 1), e1).astype(BF16)
        both = jnp.concatenate([present, jnp.zeros_like(present)], axis=0)
        SR[b, 0, 128:144, :] = pad
        SR[b, 1, 128:144, :] = pltpu.roll(both, 64, 1).astype(BF16)

    def left_part(part):
        return slice(0, PART) if part == 0 else slice(PART, 144)

    def left_out(k, h, part):
        b = block_of(k)
        c = rc(
            SL.at[b, h, left_part(part)], RL.at[b // 4, x, core, left_part(part)],
            a_ss.at[part, k, h], a_rl.at[part, b // 4, x, core],
            (yh * 4 + lax.rem(b, 4), cc * 2 + h),
        )
        return c, jnp.logical_and(lax.rem(b, 4) == x, h == core)

    def right_out(k, h):
        b = block_of(k)
        c = rc(
            SR.at[b, h], RR.at[cc, core], a_ss.at[2, k, h], a_rr.at[cc, core], (row, b * 2 + h)
        )
        return c, jnp.logical_and(b == cc, h == core)

    def each(make, k, wait):
        for h in range(2):
            c, mine = make(k, h)

            @pl.when(jnp.logical_not(mine))
            def _():
                c.wait_send() if wait else c.start()

    def every(make, wait):
        lax.fori_loop(0, 8, lambda k, _: (each(make, k, wait), 0)[1], 0)

    def send_block(k):
        each(lambda k, h: left_out(k, h, 0), k, False)
        each(right_out, k, False)

    def project_and_send(k, _):
        project(k)
        send_block(k)
        return 0

    project(0)
    pl.semaphore_wait(bar, len(greeted))
    send_block(0)
    lax.fori_loop(1, 8, project_and_send, 0)

    def start():
        for i in range(2):
            RL[i, x, core] = SL[i * 4 + x, core]
        RR[cc, core] = SR[cc, core]

    def prepare():
        for c in loads[5:8]:
            c.wait()
        for g in range(8):
            WT[:, g * 128:(g + 1) * 128] = jnp.transpose(
                wout[g * 128:(g + 1) * 128, :].astype(F32)
            ).astype(BF16)
        bT[...] = jnp.transpose(
            jnp.concatenate([bias[...], jnp.zeros((126, 128), F32)], axis=0)
        )
        T[0:128, :] = jnp.transpose(
            jnp.broadcast_to(chain[pl.ds(cc, 1), :].astype(F32), (128, 128))
        )
        SM[...] = jnp.where(
            T[pl.ds(pl.multiple_of(core * 64, 64), 64), :] == chain[pl.ds(row, 1), :].astype(F32),
            1.0, 0.0,
        )

        def clear(i, _):
            acc[i] = jnp.zeros((128, 256), F32)
            return 0

        lax.fori_loop(0, 32, clear, 0)

    m_own = yl * 4 + z

    def rows_at(m):
        return pl.ds(pl.multiple_of(m * 16, 16), 16)

    def left_in(part):
        for i in range(2):
            for n in range(4):
                for k in range(2):
                    @pl.when(jnp.logical_not(jnp.logical_and(n == x, k == core)))
                    def _():
                        ref = RL.at[i, n, k, left_part(part)]
                        rc(ref, ref, a_ss.at[0, 0, 0], a_rl.at[part, i, n, k], (row, col)).wait_recv()

    def joined(i, n, at):
        a = RL[i, n, 0, at:at + 16, :].astype(F32)
        b = RL[i, n, 1, at:at + 16, :].astype(F32)
        return [
            jnp.concatenate([a[8 * u:8 * u + 8], b[8 * u:8 * u + 8]], axis=0).astype(BF16)
            for u in range(2)
        ]

    def join_groups(gs):
        def one(n, _):
            for g in gs:
                for u, v in enumerate(joined(yh, n, 16 * g + 16)):
                    L[core, 2 * g + u, yh * 4 + n, rows_at(m_own), :] = v
                for u, v in enumerate(joined(1 - yh, n, 16 * g + 16)):
                    LX[2 * g + u, n] = v
            return 0

        lax.fori_loop(0, 4, one, 0)

    sibling = dev(yh, x, yl, z, 1 - core)

    def turn():
        for m in range(8):
            for k in range(2):
                @pl.when(jnp.logical_not(jnp.logical_and(m == cc, k == core)))
                def _():
                    ref = RR.at[m, k]
                    rc(ref, ref, a_ss.at[0, 0, 0], a_rr.at[m, k], (row, col)).wait_recv()
        for g in range(8):
            parts = [
                RR[m, k, 16 * g:16 * g + 16, :].astype(F32) for m in range(8) for k in range(2)
            ]
            for u in range(2):
                t = jnp.transpose(
                    jnp.concatenate([p[8 * u:8 * u + 8] for p in parts], axis=0)
                )
                for i in range(2):
                    T[pl.ds(4 * g + 2 * u + i, 64, stride=32), :] = t[64 * i:64 * i + 64]
        R[row, 2:66] = T[...].astype(BF16).reshape(64, 32, 128)
        t = jnp.transpose(jnp.concatenate(
            [RR[m, k, 128:144, :].astype(F32)[0:8] for m in range(8) for k in range(2)], axis=0
        ))
        R[row, 0:2] = t[0:64].astype(BF16).reshape(2, 32, 128)

    sends = []

    ALL = slice(None)

    def l_regions(q, h, m, part=None, yhalf=None):
        lo, num = 2 * LEFT[q][0], 2 * LEFT[q][1]
        if part is not None:
            num //= 2
            lo += part * num
        n = ALL if yhalf is None else pl.ds(yhalf * 4, 4)
        regions = [(q, L.at[h, lo:lo + num, n, rows_at(m), :])]
        if q == MQ:
            i = part if part is not None else ALL if yhalf is None else yhalf
            regions.append((Q, Lm.at[i, pl.ds(h * 2, 2), rows_at(m), :]))
        return regions

    def l_send(q, m, to, slot, **which):
        for i, ref in l_regions(q, core, m, **which):
            c = rc(ref, ref, l_ss.at[i, slot], l_rs.at[i, slot], to)
            c.start()
            sends.append(c)

    def l_recv(q, h, m, slot, **which):
        for i, ref in l_regions(q, h, m, **which):
            rc(ref, ref, l_ss.at[i, slot], l_rs.at[i, slot], (row, col)).wait_recv()

    def r_region(p, n, half):
        lo, num = RIGHT[p][0] + 2, RIGHT[p][1]
        if p == 0:
            lo, num = 0, num + 2
        if half is not None:
            num //= 2
            lo += half * num
        return R.at[n, lo:lo + num]

    def r_send(p, n, half, to, slot):
        ref = r_region(p, n, half)
        c = rc(ref, ref, r_ss.at[p, slot], r_rs.at[p, slot], to)
        c.start()
        sends.append(c)

    def r_recv(p, n, half, slot):
        ref = r_region(p, n, half)
        rc(ref, ref, r_ss.at[p, slot], r_rs.at[p, slot], (row, col)).wait_recv()

    zu, zd, zo = lax.rem(z + 1, 4), lax.rem(z + 3, 4), lax.rem(z + 2, 4)
    xu, xd, xo = lax.rem(x + 1, 4), lax.rem(x + 3, 4), lax.rem(x + 2, 4)
    l_up, l_down = dev(yh, x, yl, zu, core), dev(yh, x, yl, zd, core)
    l_side = dev(yh, x, 1 - yl, z, core)
    l_cross = dev(1 - yh, x, 1 - yl, z, core)
    r_up, r_down = dev(yh, xu, yl, z, core), dev(yh, xd, yl, z, core)
    r_side = dev(1 - yh, x, yl, z, core)
    ys = (yl, 1 - yl)
    hs = (yh, 1 - yh)
    mp, np_ = ys[1] * 4 + z, hs[1] * 4 + x

    def l_side_out(t):
        l_send(t, m_own, l_side, 0, yhalf=yh)
        lo, num = 2 * LEFT[t][0], 2 * LEFT[t][1]
        away = [LX.at[lo:lo + num], LXm.at[pl.ds(core * 2, 2)]]
        for src, (i, dst) in zip(away, l_regions(t, core, m_own, yhalf=yh)):
            c = rc(src, dst, l_ss.at[i, 17], l_rs.at[i, 17], l_cross)
            c.start()
            sends.append(c)

    def l_pass(t):
        l_recv(t, core, mp, 17, yhalf=1 - yh)
        l_send(t, mp, l_side, 18, yhalf=1 - yh)

    def r_side_out(t):
        r_send(t, row, None, r_side, 0)

    def l_own(t):
        l_send(t, m_own, l_up, 1, yhalf=yh)
        l_send(t, m_own, l_down, 2, yhalf=yh)
        l_send(t, m_own, sibling, 9, yhalf=yh)

    def l_own_rest(t):
        l_recv(t, core, m_own, 18, yhalf=1 - yh)
        l_send(t, m_own, l_up, 19, yhalf=1 - yh)
        l_send(t, m_own, l_down, 20, yhalf=1 - yh)
        l_send(t, m_own, sibling, 21, yhalf=1 - yh)

    def r_own(t):
        r_send(t, row, None, r_up, 1)
        r_send(t, row, None, r_down, 2)

    def l_partner(t):
        l_recv(t, core, mp, 0, yhalf=yh)
        l_send(t, mp, l_up, 3)
        l_send(t, mp, l_down, 4)
        l_send(t, mp, sibling, 10)

    def r_partner(t):
        r_recv(t, np_, None, 0)
        r_send(t, np_, None, r_up, 3)
        r_send(t, np_, None, r_down, 4)

    def l_near(t, m, slot, rest, w):
        if w:
            l_recv(t, core, m, slot + 2)
        else:
            l_recv(t, core, m, slot, yhalf=yh)
            l_recv(t, core, m, rest, yhalf=1 - yh)

    def l_far(t, w):
        lu, ld = ys[w] * 4 + zu, ys[w] * 4 + zd
        l_near(t, ld, 1, 19, w)
        l_send(t, ld, l_up, 5 + 2 * w, part=0)
        l_near(t, lu, 2, 20, w)
        l_send(t, lu, l_down, 6 + 2 * w, part=1)
        l_send(t, ld, sibling, 11 + 2 * w)
        l_send(t, lu, sibling, 12 + 2 * w)

    def r_far(t, w):
        ru, rd = hs[w] * 4 + xu, hs[w] * 4 + xd
        r_recv(t, rd, None, 1 + 2 * w)
        r_send(t, rd, 0, r_up, 5 + 2 * w)
        r_recv(t, ru, None, 2 + 2 * w)
        r_send(t, ru, 1, r_down, 6 + 2 * w)

    def l_last(t):
        for w in range(2):
            lo = ys[w] * 4 + zo
            l_recv(t, core, lo, 5 + 2 * w, part=0)
            l_recv(t, core, lo, 6 + 2 * w, part=1)
            l_send(t, lo, sibling, 15 + w)

    def r_done(t):
        for w in range(2):
            ro = hs[w] * 4 + xo
            r_recv(t, ro, 0, 5 + 2 * w)
            r_recv(t, ro, 1, 6 + 2 * w)

    def l_done(t):
        l_recv(t, 1 - core, m_own, 9, yhalf=yh)
        l_recv(t, 1 - core, m_own, 21, yhalf=1 - yh)
        l_recv(t, 1 - core, mp, 10)
        for w in range(2):
            l_recv(t, 1 - core, ys[w] * 4 + zd, 11 + 2 * w)
            l_recv(t, 1 - core, ys[w] * 4 + zu, 12 + 2 * w)
            l_recv(t, 1 - core, ys[w] * 4 + zo, 15 + w)

    def unit(g0, ng, j0, nj):
        lhs = jnp.concatenate(
            [R[n, pl.ds(2 + j0, nj)].reshape(nj * 32, 128) for n in range(8)], axis=1
        )
        for s0 in range(0, ng, 2):
            sn = min(2, ng - s0)
            prods = []
            for gi in range(sn):
                for h in range(2):
                    rhs = jnp.concatenate(
                        [L[h, (g0 + s0 + gi) * 2 + u].reshape(1024, 128) for u in range(2)], axis=1
                    )
                    prods.append(jnp.dot(lhs, rhs, preferred_element_type=F32).astype(BF16))
            w = WT[:, (g0 + s0) * 128:(g0 + s0 + sn) * 128]
            for jp in range(nj // 2):
                blk = jnp.concatenate(
                    [
                        jnp.concatenate(
                            [
                                o[j * 32:(j + 1) * 32, u * 128:(u + 1) * 128]
                                for o in prods for u in range(2)
                            ],
                            axis=0,
                        )
                        for j in (2 * jp, 2 * jp + 1)
                    ],
                    axis=1,
                )
                acc[j0 // 2 + jp] += jnp.dot(w, blk, preferred_element_type=F32)

    def counts():
        total = jnp.zeros((64, 128), F32)
        for n in range(8):
            total = total + jnp.dot(
                R[n, 0:2].reshape(64, 128), Lm[n // 4, n % 4], preferred_element_type=F32
            )
        CT[...] = 1.0 / (total + 0.001)

    def finish(p):
        for jp in range(CJ // 2):
            for u in range(2):
                j = 2 * jp + u
                a = acc[p * (CJ // 2) + jp, :, u * 128:(u + 1) * 128]
                a = a * CT[p * CJ + j:p * CJ + j + 1, :]
                same = SM[p * CJ + j:p * CJ + j + 1, :] > 0.5
                a = a + jnp.where(same, bT[:, 0:1], bT[:, 1:2])
                T[pl.ds(j, 128, stride=CJ), :] = jnp.transpose(a)
        cols = slice(p * CJ, (p + 1) * CJ)
        out[:, cols, :] = (
            T[...].reshape(128, CJ, 128) + pair_v[:, cols, :].astype(F32)
        ).astype(BF16)

    def join_first():
        left_in(0)
        join_groups((0, 1))
        for i in range(2):
            n = core * 2 + i
            Lm[yh, n, rows_at(m_own), :] = joined(yh, n, 0)[0]
            LXm[n] = joined(1 - yh, n, 0)[0]

    def join_rest():
        left_in(1)
        join_groups((2, 3, 4, 5, 6, 7))

    def finish_from(p):
        if not finished:
            counts()
            loads[8].wait()
        finished.append(p)
        finish(p)

    finished = []
    once = {
        "start": start, "prep": prepare, "join0": join_first, "join1": join_rest,
        "turn": turn,
        "al1out": lambda: every(lambda k, h: left_out(k, h, 1), False),
    }
    steps = {
        "lS": l_side_out, "lR": l_pass, "lO": l_own, "lP": l_partner, "lB": l_own_rest,
        "lL": l_last, "lZ": l_done,
        "lG": lambda t: l_far(t, 0), "lH": lambda t: l_far(t, 1),
        "rS": r_side_out, "rO": r_own, "rP": r_partner, "rZ": r_done,
        "rG": lambda t: r_far(t, 0), "rH": lambda t: r_far(t, 1),
    }
    for name in ORDER:
        if name in once:
            once[name]()
        elif name[0] == "u":
            unit(*[int(v) for v in name[1:].split(".")])
        elif name[0] == "f":
            finish_from(int(name[1:]))
        else:
            steps[name[:2]](int(name[2:]))

    for c in sends:
        c.wait_send()
    every(lambda k, h: left_out(k, h, 0), True)
    every(right_out, True)
    every(lambda k, h: left_out(k, h, 1), True)


def per_device(
    homolog_features,
    presence_flags,
    residue_chain_index,
    pair_state,
    standardize_scale,
    standardize_shift,
    left_factor_matrix,
    right_factor_matrix,
    output_weight,
    chain_pair_bias,
):
    anywhere = pl.BlockSpec(memory_space=pl.ANY)
    dma = pltpu.SemaphoreType.DMA
    return pl.pallas_call(
        kernel,
        out_shape=pltpu.VMEM(pair_state.shape, BF16),
        in_specs=[anywhere] * 10,
        out_specs=pl.BlockSpec(memory_space=pltpu.VMEM),
        scratch_shapes=[
            pltpu.VMEM((8, 8, 128, 256), BF16),
            pltpu.VMEM((512, 128), F32),
            pltpu.VMEM((8, 2, 144, 128), BF16),
            pltpu.VMEM((8, 2, 144, 128), BF16),
            pltpu.VMEM((2, 4, 2, 144, 128), BF16),
            pltpu.VMEM((8, 2, 144, 128), BF16),
            pltpu.VMEM((2, 16, 8, 128, 128), BF16),
            pltpu.VMEM((2, 4, 128, 128), BF16),
            pltpu.VMEM((16, 4, 16, 128), BF16),
            pltpu.VMEM((4, 16, 128), BF16),
            pltpu.VMEM((8, 66, 32, 128), BF16),
            pltpu.VMEM((2048, 128), F32),
            pltpu.VMEM((128, 1024), BF16),
            pltpu.VMEM((64, 256), BF16),
            pltpu.VMEM((32, 128, 256), F32),
            pltpu.VMEM((64, 128), F32),
            pltpu.VMEM((64, 128), F32),
            pltpu.VMEM((128, 64, 128), BF16),
            pltpu.VMEM((128, 128), F32),
            pltpu.VMEM((8, 1024), jnp.int32),
            pltpu.VMEM((8, 128), jnp.int32),
            pltpu.VMEM((1, 256), F32),
            pltpu.VMEM((1, 256), F32),
            pltpu.VMEM((1024, 128), BF16),
            pltpu.VMEM((2, 128), F32),
            dma((8,)), dma((9,)),
            dma((3, 8, 2)), dma((2, 2, 4, 2)), dma((8, 2)),
            dma((Q + 1, 22)), dma((Q + 1, 22)), dma((P, 9)), dma((P, 9)),
        ],
        compiler_params=pltpu.CompilerParams(
            collective_id=0, has_side_effects=True, vmem_limit_bytes=61 << 20
        ),
    )(
        homolog_features, presence_flags, residue_chain_index.reshape(8, 128),
        pair_state, standardize_scale.reshape(1, -1),
        standardize_shift.reshape(1, -1), left_factor_matrix.T, right_factor_matrix.T,
        output_weight, chain_pair_bias,
    )


def solution(mesh):
    return jax.shard_map(
        per_device,
        mesh=mesh,
        in_specs=(
            Spec(("row", "col"), None, None),
            Spec(("row", "col"), None),
            Spec(),
            Spec("row", "col", None),
            Spec(),
            Spec(),
            Spec(),
            Spec(),
            Spec(),
            Spec(),
        ),
        out_specs=Spec("row", "col", None),
        check_vma=False,
    )
```

```python
import jax
import jax.numpy as jnp
from jax import lax
from jax.experimental import pallas as pl
from jax.experimental.pallas import tpu as pltpu
from jax.sharding import PartitionSpec as Spec

MESH = pl.DeviceIdType.MESH
F32 = jnp.float32
BF16 = jnp.bfloat16
LEFT = ((0, 2), (2, 2), (4, 2), (6, 2))
RIGHT = ((0, 16), (16, 16), (32, 16), (48, 16))
ORDER = (
    "start", "prep", "al1out", "join0", "lS0", "lO0", "turn", "rS0", "rO0", "lR0", "lP0",
    "join1", "lO1", "lS1", "rO2", "lH0", "rP0", "rG0", "rS1", "lB0", "lR1", "rG2", "lP1", "lG0",
    "rP1", "rH0", "rO1", "rS2", "lB1", "lH1", "lS2", "lO2", "lL0", "rP2", "lG1", "rH1", "lR2",
    "lP2", "lS3", "lZ0", "rZ0", "u0.2.0.16", "lL1", "rG1", "rS3", "lB2", "lR3", "lP3", "lH2",
    "rH2", "rO3", "lZ1", "u2.2.0.16", "lG2", "lO3", "rP3", "rZ1", "u2.2.16.16", "lB3", "lH3",
    "rZ2", "u0.2.32.16", "u2.2.32.16", "lL2", "u0.2.16.16", "rG3", "lG3", "rH3", "lZ2",
    "u4.2.32.16", "u4.2.16.16", "u4.2.0.16", "rZ3", "lL3", "u0.2.48.16", "u2.2.48.16",
    "u4.2.48.16", "lZ3", "u6.2.32.16", "u6.2.0.16", "f0", "f2", "u6.2.48.16", "f3",
    "u6.2.16.16", "f1",
)
Q, P = len(LEFT), len(RIGHT)
MQ = 1
PART = 48
CJ = 16


def kernel(
    feats, flags_h, chain_h, pair, scale_h, shift_h, wl, wr, wout_h, bias_h,
    out,
    F, Y, SL, SR, RL, RR, L, Lm, LX, LXm, R, T, WT, PT, acc, CT, SM, pair_v, bT,
    flags, chain, scale, shift, wout, bias,
    f_sem, i_sem, a_ss, a_rl, a_rr, l_ss, l_rs, r_ss, r_rs,
):
    row = lax.axis_index("row")
    col = lax.axis_index("col")
    yh, x = row // 4, row % 4
    cc, core = col // 2, col % 2
    yl, z = cc // 4, cc % 4

    def dev(yh_, x_, yl_, z_, k_):
        return (yh_ * 4 + x_, yl_ * 8 + z_ * 2 + k_)

    def rc(src, dst, ss, rs, d):
        return pltpu.make_async_remote_copy(
            src_ref=src, dst_ref=dst, send_sem=ss, recv_sem=rs, device_id=d, device_id_type=MESH
        )

    bar = pltpu.get_barrier_semaphore()
    greeted = [(row, lax.rem(col + d, 16)) for d in range(1, 16)]
    greeted += [
        (yh * 4 + lax.rem(x + d, 4), cc * 2 + k) for d in range(1, 4) for k in range(2)
    ]
    greeted += [dev(1 - yh, x, yl, z, core), dev(1 - yh, x, 1 - yl, z, core)]
    for d in greeted:
        pl.semaphore_signal(bar, inc=1, device_id=d, device_id_type=MESH)

    def block_of(k):
        return lax.rem(row + cc + k, 8)

    def f_copy(k):
        b = block_of(k)
        return pltpu.make_async_copy(
            feats.at[:, pl.ds(pl.multiple_of(b * 128, 128), 128), :], F.at[k], f_sem.at[k]
        )

    loads = [
        pltpu.make_async_copy(src, dst, i_sem.at[i])
        for i, (src, dst) in enumerate((
            (flags_h, flags), (scale_h, scale), (shift_h, shift),
            (wl, PT.at[0:32]), (wr, PT.at[32:64]),
            (wout_h, wout), (bias_h, bias), (chain_h, chain), (pair, pair_v),
        ))
    ]
    for c in loads[:5]:
        c.start()
    for k in range(8):
        f_copy(k).start()
    for c in loads[5:]:
        c.start()
    for c in loads[:5]:
        c.wait()

    def project(k):
        f_copy(k).wait()
        b = block_of(k)
        present = flags[:, pl.ds(pl.multiple_of(b * 128, 128), 128)].astype(F32)
        for sp in range(4):
            v = F[k, 2 * sp:2 * sp + 2].reshape(256, 256).astype(F32)
            mu = jnp.mean(v, axis=-1, keepdims=True)
            d = v - mu
            var = jnp.mean(d * d, axis=-1, keepdims=True)
            nrm = (d * lax.rsqrt(var + 1e-05) * scale[...] + shift[...]).astype(BF16)
            pr = lax.dot_general(
                PT[...], nrm, (((1,), (1,)), ((), ())), preferred_element_type=F32
            )
            for u in range(2):
                s = 2 * sp + u
                Y[pl.ds(s, 64, stride=8), :] = pr[:, u * 128:(u + 1) * 128] * present[s:s + 1, :]
        pad = jnp.concatenate([present, jnp.zeros_like(present)], axis=0).astype(BF16)
        for h in range(2):
            SL[b, h, 0:16, :] = pad
            for g in range(8):
                at = (4 * g + 2 * h) * 8
                SL[b, h, 16 * g + 16:16 * g + 32, :] = Y[at:at + 16, :].astype(BF16)
        low = lax.broadcasted_iota(jnp.int32, (16, 128), 1) < 64
        for g in range(8):
            y = Y[256 + 32 * g:288 + 32 * g, :]
            e0 = jnp.concatenate([y[0:8], y[16:24]], axis=0)
            e1 = jnp.concatenate([y[8:16], y[24:32]], axis=0)
            at = slice(16 * g, 16 * g + 16)
            SR[b, 0, at, :] = jnp.where(low, e0, pltpu.roll(e1, 64, 1)).astype(BF16)
            SR[b, 1, at, :] = jnp.where(low, pltpu.roll(e0, 64, 1), e1).astype(BF16)
        both = jnp.concatenate([present, jnp.zeros_like(present)], axis=0)
        SR[b, 0, 128:144, :] = pad
        SR[b, 1, 128:144, :] = pltpu.roll(both, 64, 1).astype(BF16)

    def left_part(part):
        return slice(0, PART) if part == 0 else slice(PART, 144)

    def left_out(k, h, part):
        b = block_of(k)
        c = rc(
            SL.at[b, h, left_part(part)], RL.at[b // 4, x, core, left_part(part)],
            a_ss.at[part, k, h], a_rl.at[part, b // 4, x, core],
            (yh * 4 + lax.rem(b, 4), cc * 2 + h),
        )
        return c, jnp.logical_and(lax.rem(b, 4) == x, h == core)

    def right_out(k, h):
        b = block_of(k)
        c = rc(
            SR.at[b, h], RR.at[cc, core], a_ss.at[2, k, h], a_rr.at[cc, core], (row, b * 2 + h)
        )
        return c, jnp.logical_and(b == cc, h == core)

    def each(make, k, wait):
        for h in range(2):
            c, mine = make(k, h)

            @pl.when(jnp.logical_not(mine))
            def _():
                c.wait_send() if wait else c.start()

    def every(make, wait):
        lax.fori_loop(0, 8, lambda k, _: (each(make, k, wait), 0)[1], 0)

    def send_block(k):
        each(lambda k, h: left_out(k, h, 0), k, False)
        each(right_out, k, False)

    def project_and_send(k, _):
        project(k)
        send_block(k)
        return 0

    project(0)
    pl.semaphore_wait(bar, len(greeted))
    send_block(0)
    lax.fori_loop(1, 8, project_and_send, 0)

    def start():
        for i in range(2):
            RL[i, x, core] = SL[i * 4 + x, core]
        RR[cc, core] = SR[cc, core]

    def prepare():
        for c in loads[5:8]:
            c.wait()
        for g in range(8):
            WT[:, g * 128:(g + 1) * 128] = jnp.transpose(
                wout[g * 128:(g + 1) * 128, :].astype(F32)
            ).astype(BF16)
        bT[...] = jnp.transpose(
            jnp.concatenate([bias[...], jnp.zeros((126, 128), F32)], axis=0)
        )
        T[0:128, :] = jnp.transpose(
            jnp.broadcast_to(chain[pl.ds(cc, 1), :].astype(F32), (128, 128))
        )
        SM[...] = jnp.where(
            T[pl.ds(pl.multiple_of(core * 64, 64), 64), :] == chain[pl.ds(row, 1), :].astype(F32),
            1.0, 0.0,
        )

        def clear(i, _):
            acc[i] = jnp.zeros((128, 256), F32)
            return 0

        lax.fori_loop(0, 32, clear, 0)

    m_own = yl * 4 + z

    def rows_at(m):
        return pl.ds(pl.multiple_of(m * 16, 16), 16)

    def left_in(part):
        for i in range(2):
            for n in range(4):
                for k in range(2):
                    @pl.when(jnp.logical_not(jnp.logical_and(n == x, k == core)))
                    def _():
                        ref = RL.at[i, n, k, left_part(part)]
                        rc(ref, ref, a_ss.at[0, 0, 0], a_rl.at[part, i, n, k], (row, col)).wait_recv()

    def joined(i, n, at):
        a = RL[i, n, 0, at:at + 16, :].astype(F32)
        b = RL[i, n, 1, at:at + 16, :].astype(F32)
        return [
            jnp.concatenate([a[8 * u:8 * u + 8], b[8 * u:8 * u + 8]], axis=0).astype(BF16)
            for u in range(2)
        ]

    def join_groups(gs):
        def one(n, _):
            for g in gs:
                for u, v in enumerate(joined(yh, n, 16 * g + 16)):
                    L[core, 2 * g + u, yh * 4 + n, rows_at(m_own), :] = v
                for u, v in enumerate(joined(1 - yh, n, 16 * g + 16)):
                    LX[2 * g + u, n] = v
            return 0

        lax.fori_loop(0, 4, one, 0)

    sibling = dev(yh, x, yl, z, 1 - core)

    def turn():
        for m in range(8):
            for k in range(2):
                @pl.when(jnp.logical_not(jnp.logical_and(m == cc, k == core)))
                def _():
                    ref = RR.at[m, k]
                    rc(ref, ref, a_ss.at[0, 0, 0], a_rr.at[m, k], (row, col)).wait_recv()
        for g in range(8):
            parts = [
                RR[m, k, 16 * g:16 * g + 16, :].astype(F32) for m in range(8) for k in range(2)
            ]
            for u in range(2):
                t = jnp.transpose(
                    jnp.concatenate([p[8 * u:8 * u + 8] for p in parts], axis=0)
                )
                for i in range(2):
                    T[pl.ds(4 * g + 2 * u + i, 64, stride=32), :] = t[64 * i:64 * i + 64]
        R[row, 2:66] = T[...].astype(BF16).reshape(64, 32, 128)
        t = jnp.transpose(jnp.concatenate(
            [RR[m, k, 128:144, :].astype(F32)[0:8] for m in range(8) for k in range(2)], axis=0
        ))
        R[row, 0:2] = t[0:64].astype(BF16).reshape(2, 32, 128)

    sends = []

    ALL = slice(None)

    def l_regions(q, h, m, part=None, yhalf=None):
        lo, num = 2 * LEFT[q][0], 2 * LEFT[q][1]
        if part is not None:
            num //= 2
            lo += part * num
        n = ALL if yhalf is None else pl.ds(yhalf * 4, 4)
        regions = [(q, L.at[h, lo:lo + num, n, rows_at(m), :])]
        if q == MQ:
            i = part if part is not None else ALL if yhalf is None else yhalf
            regions.append((Q, Lm.at[i, pl.ds(h * 2, 2), rows_at(m), :]))
        return regions

    def l_send(q, m, to, slot, **which):
        for i, ref in l_regions(q, core, m, **which):
            c = rc(ref, ref, l_ss.at[i, slot], l_rs.at[i, slot], to)
            c.start()
            sends.append(c)

    def l_recv(q, h, m, slot, **which):
        for i, ref in l_regions(q, h, m, **which):
            rc(ref, ref, l_ss.at[i, slot], l_rs.at[i, slot], (row, col)).wait_recv()

    def r_region(p, n, half):
        lo, num = RIGHT[p][0] + 2, RIGHT[p][1]
        if p == 0:
            lo, num = 0, num + 2
        if half is not None:
            num //= 2
            lo += half * num
        return R.at[n, lo:lo + num]

    def r_send(p, n, half, to, slot):
        ref = r_region(p, n, half)
        c = rc(ref, ref, r_ss.at[p, slot], r_rs.at[p, slot], to)
        c.start()
        sends.append(c)

    def r_recv(p, n, half, slot):
        ref = r_region(p, n, half)
        rc(ref, ref, r_ss.at[p, slot], r_rs.at[p, slot], (row, col)).wait_recv()

    zu, zd, zo = lax.rem(z + 1, 4), lax.rem(z + 3, 4), lax.rem(z + 2, 4)
    xu, xd, xo = lax.rem(x + 1, 4), lax.rem(x + 3, 4), lax.rem(x + 2, 4)
    l_up, l_down = dev(yh, x, yl, zu, core), dev(yh, x, yl, zd, core)
    l_side = dev(yh, x, 1 - yl, z, core)
    l_cross = dev(1 - yh, x, 1 - yl, z, core)
    r_up, r_down = dev(yh, xu, yl, z, core), dev(yh, xd, yl, z, core)
    r_side = dev(1 - yh, x, yl, z, core)
    ys = (yl, 1 - yl)
    hs = (yh, 1 - yh)
    mp, np_ = ys[1] * 4 + z, hs[1] * 4 + x

    def l_side_out(t):
        l_send(t, m_own, l_side, 0, yhalf=yh)
        lo, num = 2 * LEFT[t][0], 2 * LEFT[t][1]
        away = [LX.at[lo:lo + num], LXm.at[pl.ds(core * 2, 2)]]
        for src, (i, dst) in zip(away, l_regions(t, core, m_own, yhalf=yh)):
            c = rc(src, dst, l_ss.at[i, 17], l_rs.at[i, 17], l_cross)
            c.start()
            sends.append(c)

    def l_pass(t):
        l_recv(t, core, mp, 17, yhalf=1 - yh)
        l_send(t, mp, l_side, 18, yhalf=1 - yh)

    def r_side_out(t):
        r_send(t, row, None, r_side, 0)

    def l_own(t):
        l_send(t, m_own, l_up, 1, yhalf=yh)
        l_send(t, m_own, l_down, 2, yhalf=yh)
        l_send(t, m_own, sibling, 9, yhalf=yh)

    def l_own_rest(t):
        l_recv(t, core, m_own, 18, yhalf=1 - yh)
        l_send(t, m_own, l_up, 19, yhalf=1 - yh)
        l_send(t, m_own, l_down, 20, yhalf=1 - yh)
        l_send(t, m_own, sibling, 21, yhalf=1 - yh)

    def r_own(t):
        r_send(t, row, None, r_up, 1)
        r_send(t, row, None, r_down, 2)

    def l_partner(t):
        l_recv(t, core, mp, 0, yhalf=yh)
        l_send(t, mp, l_up, 3)
        l_send(t, mp, l_down, 4)
        l_send(t, mp, sibling, 10)

    def r_partner(t):
        r_recv(t, np_, None, 0)
        r_send(t, np_, None, r_up, 3)
        r_send(t, np_, None, r_down, 4)

    def l_near(t, m, slot, rest, w):
        if w:
            l_recv(t, core, m, slot + 2)
        else:
            l_recv(t, core, m, slot, yhalf=yh)
            l_recv(t, core, m, rest, yhalf=1 - yh)

    def l_far(t, w):
        lu, ld = ys[w] * 4 + zu, ys[w] * 4 + zd
        l_near(t, ld, 1, 19, w)
        l_send(t, ld, l_up, 5 + 2 * w, part=0)
        l_near(t, lu, 2, 20, w)
        l_send(t, lu, l_down, 6 + 2 * w, part=1)
        l_send(t, ld, sibling, 11 + 2 * w)
        l_send(t, lu, sibling, 12 + 2 * w)

    def r_far(t, w):
        ru, rd = hs[w] * 4 + xu, hs[w] * 4 + xd
        r_recv(t, rd, None, 1 + 2 * w)
        r_send(t, rd, 0, r_up, 5 + 2 * w)
        r_recv(t, ru, None, 2 + 2 * w)
        r_send(t, ru, 1, r_down, 6 + 2 * w)

    def l_last(t):
        for w in range(2):
            lo = ys[w] * 4 + zo
            l_recv(t, core, lo, 5 + 2 * w, part=0)
            l_recv(t, core, lo, 6 + 2 * w, part=1)
            l_send(t, lo, sibling, 15 + w)

    def r_done(t):
        for w in range(2):
            ro = hs[w] * 4 + xo
            r_recv(t, ro, 0, 5 + 2 * w)
            r_recv(t, ro, 1, 6 + 2 * w)

    def l_done(t):
        l_recv(t, 1 - core, m_own, 9, yhalf=yh)
        l_recv(t, 1 - core, m_own, 21, yhalf=1 - yh)
        l_recv(t, 1 - core, mp, 10)
        for w in range(2):
            l_recv(t, 1 - core, ys[w] * 4 + zd, 11 + 2 * w)
            l_recv(t, 1 - core, ys[w] * 4 + zu, 12 + 2 * w)
            l_recv(t, 1 - core, ys[w] * 4 + zo, 15 + w)

    def unit(g0, ng, j0, nj):
        lhs = jnp.concatenate(
            [R[n, pl.ds(2 + j0, nj)].reshape(nj * 32, 128) for n in range(8)], axis=1
        )
        for s0 in range(0, ng, 2):
            sn = min(2, ng - s0)
            prods = []
            for gi in range(sn):
                for h in range(2):
                    rhs = jnp.concatenate(
                        [L[h, (g0 + s0 + gi) * 2 + u].reshape(1024, 128) for u in range(2)], axis=1
                    )
                    prods.append(jnp.dot(lhs, rhs, preferred_element_type=F32).astype(BF16))
            w = WT[:, (g0 + s0) * 128:(g0 + s0 + sn) * 128]
            for jp in range(nj // 2):
                blk = jnp.concatenate(
                    [
                        jnp.concatenate(
                            [
                                o[j * 32:(j + 1) * 32, u * 128:(u + 1) * 128]
                                for o in prods for u in range(2)
                            ],
                            axis=0,
                        )
                        for j in (2 * jp, 2 * jp + 1)
                    ],
                    axis=1,
                )
                acc[j0 // 2 + jp] += jnp.dot(w, blk, preferred_element_type=F32)

    def counts():
        total = jnp.zeros((64, 128), F32)
        for n in range(8):
            total = total + jnp.dot(
                R[n, 0:2].reshape(64, 128), Lm[n // 4, n % 4], preferred_element_type=F32
            )
        CT[...] = 1.0 / (total + 0.001)

    def finish(p):
        for jp in range(CJ // 2):
            for u in range(2):
                j = 2 * jp + u
                a = acc[p * (CJ // 2) + jp, :, u * 128:(u + 1) * 128]
                a = a * CT[p * CJ + j:p * CJ + j + 1, :]
                same = SM[p * CJ + j:p * CJ + j + 1, :] > 0.5
                a = a + jnp.where(same, bT[:, 0:1], bT[:, 1:2])
                T[pl.ds(j, 128, stride=CJ), :] = jnp.transpose(a)
        cols = slice(p * CJ, (p + 1) * CJ)
        out[:, cols, :] = (
            T[...].reshape(128, CJ, 128) + pair_v[:, cols, :].astype(F32)
        ).astype(BF16)

    def join_first():
        left_in(0)
        join_groups((0, 1))
        for i in range(2):
            n = core * 2 + i
            Lm[yh, n, rows_at(m_own), :] = joined(yh, n, 0)[0]
            LXm[n] = joined(1 - yh, n, 0)[0]

    def join_rest():
        left_in(1)
        join_groups((2, 3, 4, 5, 6, 7))

    def finish_from(p):
        if not finished:
            counts()
            loads[8].wait()
        finished.append(p)
        finish(p)

    finished = []
    once = {
        "start": start, "prep": prepare, "join0": join_first, "join1": join_rest,
        "turn": turn,
        "al1out": lambda: every(lambda k, h: left_out(k, h, 1), False),
    }
    steps = {
        "lS": l_side_out, "lR": l_pass, "lO": l_own, "lP": l_partner, "lB": l_own_rest,
        "lL": l_last, "lZ": l_done,
        "lG": lambda t: l_far(t, 0), "lH": lambda t: l_far(t, 1),
        "rS": r_side_out, "rO": r_own, "rP": r_partner, "rZ": r_done,
        "rG": lambda t: r_far(t, 0), "rH": lambda t: r_far(t, 1),
    }
    for name in ORDER:
        if name in once:
            once[name]()
        elif name[0] == "u":
            unit(*[int(v) for v in name[1:].split(".")])
        elif name[0] == "f":
            finish_from(int(name[1:]))
        else:
            steps[name[:2]](int(name[2:]))

    for c in sends:
        c.wait_send()
    every(lambda k, h: left_out(k, h, 0), True)
    every(right_out, True)
    every(lambda k, h: left_out(k, h, 1), True)


def per_device(
    homolog_features,
    presence_flags,
    residue_chain_index,
    pair_state,
    standardize_scale,
    standardize_shift,
    left_factor_matrix,
    right_factor_matrix,
    output_weight,
    chain_pair_bias,
):
    anywhere = pl.BlockSpec(memory_space=pl.ANY)
    dma = pltpu.SemaphoreType.DMA
    return pl.pallas_call(
        kernel,
        out_shape=pltpu.VMEM(pair_state.shape, BF16),
        in_specs=[anywhere] * 10,
        out_specs=pl.BlockSpec(memory_space=pltpu.VMEM),
        scratch_shapes=[
            pltpu.VMEM((8, 8, 128, 256), BF16),
            pltpu.VMEM((512, 128), F32),
            pltpu.VMEM((8, 2, 144, 128), BF16),
            pltpu.VMEM((8, 2, 144, 128), BF16),
            pltpu.VMEM((2, 4, 2, 144, 128), BF16),
            pltpu.VMEM((8, 2, 144, 128), BF16),
            pltpu.VMEM((2, 16, 8, 128, 128), BF16),
            pltpu.VMEM((2, 4, 128, 128), BF16),
            pltpu.VMEM((16, 4, 16, 128), BF16),
            pltpu.VMEM((4, 16, 128), BF16),
            pltpu.VMEM((8, 66, 32, 128), BF16),
            pltpu.VMEM((2048, 128), F32),
            pltpu.VMEM((128, 1024), BF16),
            pltpu.VMEM((64, 256), BF16),
            pltpu.VMEM((32, 128, 256), F32),
            pltpu.VMEM((64, 128), F32),
            pltpu.VMEM((64, 128), F32),
            pltpu.VMEM((128, 64, 128), BF16),
            pltpu.VMEM((128, 128), F32),
            pltpu.VMEM((8, 1024), jnp.int32),
            pltpu.VMEM((8, 128), jnp.int32),
            pltpu.VMEM((1, 256), F32),
            pltpu.VMEM((1, 256), F32),
            pltpu.VMEM((1024, 128), BF16),
            pltpu.VMEM((2, 128), F32),
            dma((8,)), dma((9,)),
            dma((3, 8, 2)), dma((2, 2, 4, 2)), dma((8, 2)),
            dma((Q + 1, 22)), dma((Q + 1, 22)), dma((P, 9)), dma((P, 9)),
        ],
        compiler_params=pltpu.CompilerParams(
            collective_id=0, has_side_effects=True, vmem_limit_bytes=61 << 20
        ),
    )(
        homolog_features, presence_flags, residue_chain_index.reshape(8, 128),
        pair_state, standardize_scale.reshape(1, -1),
        standardize_shift.reshape(1, -1), left_factor_matrix.T, right_factor_matrix.T,
        output_weight, chain_pair_bias,
    )


def solution(mesh):
    return jax.shard_map(
        per_device,
        mesh=mesh,
        in_specs=(
            Spec(("row", "col"), None, None),
            Spec(("row", "col"), None),
            Spec(),
            Spec("row", "col", None),
            Spec(),
            Spec(),
            Spec(),
            Spec(),
            Spec(),
            Spec(),
        ),
        out_specs=Spec("row", "col", None),
        check_vma=False,
    )
```
